32 devices in a mesh: sec: 4 (over x, core), row: 4 (over z), col: 2 (over y).
Axes of the slice: x: 2, y: 2, z: 4, core: 2. Of those that a mesh axis runs over, the one named last changes fastest.
Arguments:
- amplitudes: bfloat16 [4, 2, 512, 8192], P('sec', None, 'row', 'col'), may hold values from -0.25 to 0.25, as said below
- state_energies: float32 [4, 8192], P('sec', 'col'), may hold values from 1.25 to 12
- radii_table: int32 [5], replicated, may hold values from 20 to 84, as said below
- plan: int32 [4, 2], P('sec'), may hold values from 0 to 31, as said below
- entry_r: float32 [4, 512, 512], P('sec', 'col', 'row'), may hold values from -16 to 48, as said below
- fresh_r: float32 [1, 512, 512], P(None, 'col', 'row'), may hold values from -16 to 48, as said below
Outputs:
- exit_r: float32 [2, 4, 512, 512], P(None, 'sec', 'col', 'row')
The draws below stay inside these ranges and needn't reach their ends.
Inputs may be any that keep to these rules, and one draw needn't show every extreme that they name: Each sector's outer-boundary amplitudes are correlated with its inner-boundary ones. `radii_table`: strictly increasing; consecutive radii differ by 4 to 16; the first is at least 20 and the last equals 84. plan[s, t] equals plan[s-1, t-1] for s, t >= 1. `entry_r`: symmetric positive definite, every eigenvalue at least 0.5. `fresh_r`: symmetric positive definite, every eigenvalue at least 0.5.
All inputs are finite; a program needn't handle non-finite values.
Results may differ from the reference program's by a relative error of at most 0.0016.
Values may be sent and summed in bfloat16 or wider, within the bound.
A program may use at most 64 MiB of HBM per device.

```python
import math
import jax
import jax.numpy as jnp
from jax import lax

N = 512
K = 8192
ENERGIES = 32
TICKS = 2
SECTORS = 4


def channel_mixer(key):
    key_left, key_right, key_gain = jax.random.split(key, 3)
    identity = jnp.eye(N, dtype=jnp.float32)
    left = identity + 0.35 * jnp.clip(jax.random.normal(key_left, (N, N), jnp.float32), -5.0, 5.0) / math.sqrt(N)
    right = identity + 0.35 * jnp.clip(jax.random.normal(key_right, (N, N), jnp.float32), -5.0, 5.0) / math.sqrt(N)
    gains = jnp.exp(jax.random.uniform(key_gain, (N,), jnp.float32, math.log(0.5), math.log(4.0)))
    return jnp.dot(left * gains[None, :], right, precision=lax.Precision.HIGHEST)


def draw_amplitudes(key, part):
    base = jax.random.fold_in(key, 11)
    key_inner = jax.random.fold_in(base, 0)
    key_other = jax.random.fold_in(base, 1)
    key_mix = jax.random.fold_in(base, 3)
    mixer = channel_mixer(key_mix)
    inner = jnp.clip(jax.random.normal(key_inner, (SECTORS, N, K), jnp.float32), -5.0, 5.0)
    other = jnp.clip(jax.random.normal(key_other, (SECTORS, N, K), jnp.float32), -5.0, 5.0)
    inner = jnp.einsum('nm,smk->snk', mixer, inner, precision=lax.Precision.HIGHEST)
    other = jnp.einsum('nm,smk->snk', mixer, other, precision=lax.Precision.HIGHEST)
    outer = 0.8 * inner + 0.6 * other
    stacked = jnp.stack([inner, outer], 1) / math.sqrt(K)
    return jnp.clip(stacked, -0.25, 0.25).astype(jnp.bfloat16)


def draw_radii_table(key, part):
    base = jax.random.fold_in(key, 23)
    widths = jax.random.randint(base, (SECTORS,), 4, 17, jnp.int32)
    outermost = 20 + 16 * SECTORS
    first = outermost - jnp.sum(widths)
    table = jnp.concatenate([first[None], first + jnp.cumsum(widths)])
    return table.astype(jnp.int32)


def draw_plan(key, part):
    base = jax.random.fold_in(key, 31)
    stream = jax.random.randint(base, (SECTORS + TICKS - 1,), 0, ENERGIES, jnp.int32)
    stream = stream.at[0].set(0)
    stream = stream.at[SECTORS + TICKS - 2].set(ENERGIES - 1)
    sector_ids = jnp.arange(SECTORS, dtype=jnp.int32)[:, None]
    period_ids = jnp.arange(TICKS, dtype=jnp.int32)[None, :]
    return stream[period_ids - sector_ids + SECTORS - 1].astype(jnp.int32)


def definite_matrices(key, count):
    key_base = jax.random.fold_in(key, 0)
    key_spread = jax.random.fold_in(key, 2)
    values = jnp.clip(jax.random.normal(key_base, (count, N, N), jnp.float32), -5.0, 5.0)
    spread = jnp.exp(jax.random.uniform(key_spread, (count, 1, N), jnp.float32, math.log(0.05), math.log(20.0)))
    gram = jnp.einsum('snm,skm->snk', values * spread, values, precision=lax.Precision.HIGHEST) / N
    gram = 0.5 * (gram + jnp.swapaxes(gram, 1, 2))
    return 0.5 * jnp.eye(N, dtype=jnp.float32)[None] + gram


def draw_entry_r(key, part):
    return definite_matrices(jax.random.fold_in(key, 41), SECTORS)


def draw_fresh_r(key, part):
    return definite_matrices(jax.random.fold_in(key, 43), TICKS - 1)


def level_of(stream_key, extent, cuts, smallest, largest):
    level = 1.0
    for position, parts in cuts:
        draws = jax.random.uniform(jax.random.fold_in(jax.random.fold_in(stream_key, 6), position), (parts,), jnp.float32, smallest / len(cuts), largest / len(cuts))
        level = level * jnp.repeat(jnp.exp(draws), extent[position] // parts).reshape((-1,) + (1,) * (len(extent) - 1 - position))
    return level


def setup_inputs(seed: int = 0) -> dict:
    arg_keys = jax.random.split(jax.random.key(seed), 7)
    amplitudes = draw_amplitudes(jax.random.fold_in(arg_keys[6], 71), 0)
    state_energies = jnp.clip(jnp.exp(math.log(12.0) - 2.261763 * jax.random.uniform(arg_keys[1], (SECTORS, K), jnp.float32) ** level_of(arg_keys[1], (SECTORS, K), ((0, 4), (1, 2)), -0.2, 0.2)), 1.25, 12.0)
    radii_table = draw_radii_table(jax.random.fold_in(arg_keys[6], 71), 0)
    plan = draw_plan(jax.random.fold_in(arg_keys[6], 71), 0)
    entry_r = draw_entry_r(jax.random.fold_in(arg_keys[6], 71), 0)
    fresh_r = draw_fresh_r(jax.random.fold_in(arg_keys[6], 71), 0)
    return {"amplitudes": amplitudes, "state_energies": state_energies, "radii_table": radii_table, "plan": plan, "entry_r": entry_r, "fresh_r": fresh_r}


def sector_pass(panels, levels, sector_width, energy, entering):
    weight = 8.0 / (sector_width * (levels - energy))
    scaled = (panels.astype(jnp.float32) * weight).astype(jnp.bfloat16)
    green_ll = jnp.dot(scaled[0].astype(jnp.float32), panels[0].T.astype(jnp.float32), preferred_element_type=jnp.float32)
    green_lr = jnp.dot(scaled[0].astype(jnp.float32), panels[1].T.astype(jnp.float32), preferred_element_type=jnp.float32)
    green_rr = jnp.dot(scaled[1].astype(jnp.float32), panels[1].T.astype(jnp.float32), preferred_element_type=jnp.float32)
    factor = jnp.linalg.cholesky(green_ll + entering)
    solved = jax.scipy.linalg.solve_triangular(factor, green_lr, lower=True)
    return green_rr - jnp.dot(solved.T, solved, precision=lax.Precision.HIGHEST)

def sector_items(items):
    return sector_pass(items[0], items[1], items[2], items[3], items[4])

def reference(amplitudes, state_energies, radii_table, plan, entry_r, fresh_r):
    widths = (radii_table[1:] - radii_table[:-1]).astype(jnp.float32)
    current = entry_r
    results = []
    for period in range(TICKS):
        energies = plan[:, period].astype(jnp.float32) / ENERGIES
        produced = lax.map(sector_items, (amplitudes, state_energies, widths, energies, current))
        results.append(produced)
        if period + 1 < TICKS:
            current = jnp.concatenate([fresh_r[period][None], produced[:-1]], 0)
    return jnp.stack(results, 0)
```

```python
import functools
import jax
import jax.numpy as jnp
from jax import lax
from jax.experimental import pallas as pl
from jax.experimental.pallas import tpu as pltpu
from jax.sharding import PartitionSpec as P

ENERGIES = 32
TICKS = 2
BLOCK = 128
SUB = 8
HIGHEST = lax.Precision.HIGHEST


def shifted_2(block, axis, distance):
    devices = range(lax.axis_size(axis))
    route = [(i - distance, i) for i in devices if i - distance in devices]
    return lax.ppermute(block, axis, route)


def inverse_factor(block):
    size = block.shape[0]
    groups = size // SUB
    sub_rows = lax.broadcasted_iota(jnp.int32, (SUB, size), 0)
    lanes = lax.broadcasted_iota(jnp.int32, (SUB, size), 1)
    left = [block[SUB * g : SUB * (g + 1), :] for g in range(groups)]
    right = [jnp.where(lanes == sub_rows + SUB * g, 1.0, 0.0) for g in range(groups)]
    done = []
    for g in range(groups):
        base = SUB * g
        u, v = left[g], right[g]
        cols = [jnp.broadcast_to(u[:, base + q : base + q + 1], (SUB, size)) for q in range(SUB)]
        scale = jnp.zeros((SUB, size), jnp.float32)
        for p in range(SUB):
            pivot = cols[p][p : p + 1, :]
            scale = jnp.where(sub_rows == p, pivot, scale)
            if p + 1 < SUB:
                f = jnp.where(sub_rows > p, cols[p] / pivot, 0.0)
                u = u - f * u[p : p + 1, :]
                v = v - f * v[p : p + 1, :]
                for q in range(p + 1, SUB):
                    cols[q] = cols[q] - f * cols[q][p : p + 1, :]
        scale = lax.rsqrt(scale)
        u = u * scale
        v = v * scale
        done.append(v)
        if g + 1 < groups:
            turned = u.T
            for h in range(g + 1, groups):
                for q in range(SUB):
                    c = jnp.broadcast_to(turned[SUB * h : SUB * (h + 1), q : q + 1], (SUB, size))
                    left[h] = left[h] - c * u[q : q + 1, :]
                    right[h] = right[h] - c * v[q : q + 1, :]
    return jnp.concatenate(done, 0)


def eliminate_kernel(ll_ref, lr_ref, rr_ref, entry_ref, out_ref, work):
    n = ll_ref.shape[0]
    blocks = n // BLOCK
    work[:n, :n] = ll_ref[...] + entry_ref[...]
    work[:n, n:] = lr_ref[...]
    work[n:, n:] = rr_ref[...]
    for k in range(blocks):
        lo, hi = k * BLOCK, (k + 1) * BLOCK
        factor = inverse_factor(work[lo:hi, lo:hi])
        solved = jnp.dot(
            factor, work[lo:hi, hi:], precision=HIGHEST, preferred_element_type=jnp.float32
        )
        for i in range(hi, 2 * n, BLOCK):
            work[i : i + BLOCK, i:] -= lax.dot_general(
                solved[:, i - hi : i - hi + BLOCK],
                solved[:, i - hi :],
                (((0,), (0,)), ((), ())),
                precision=HIGHEST,
                preferred_element_type=jnp.float32,
            )
    for i in range(blocks):
        for j in range(i, blocks):
            tile = work[n + i * BLOCK : n + (i + 1) * BLOCK, n + j * BLOCK : n + (j + 1) * BLOCK]
            out_ref[i * BLOCK : (i + 1) * BLOCK, j * BLOCK : (j + 1) * BLOCK] = tile
            if j > i:
                out_ref[j * BLOCK : (j + 1) * BLOCK, i * BLOCK : (i + 1) * BLOCK] = tile.T


def eliminate(ll, lr, rr, entry):
    n = ll.shape[0]
    return pl.pallas_call(
        eliminate_kernel,
        out_shape=jax.ShapeDtypeStruct((n, n), jnp.float32),
        in_specs=[pl.BlockSpec(memory_space=pltpu.VMEM)] * 4,
        out_specs=pl.BlockSpec(memory_space=pltpu.VMEM),
        scratch_shapes=[pltpu.VMEM((2 * n, 2 * n), jnp.float32)],
        compiler_params=pltpu.CompilerParams(vmem_limit_bytes=32 * 1024 * 1024),
        cost_estimate=pl.CostEstimate(
            flops=200 * n * n * n, bytes_accessed=20 * n * n, transcendentals=0
        ),
        name="eliminate",
    )(ll, lr, rr, entry)


def local(amplitudes, state_energies, radii_table, plan, entry_r, fresh_r):
    sec_index = lax.axis_index("sec")
    row_index = lax.axis_index("row")
    col_index = lax.axis_index("col")
    row_count = lax.axis_size("row")
    panels = lax.all_to_all(amplitudes[0], "row", split_axis=2, concat_axis=1, tiled=True)
    channels, states = panels.shape[1:]
    row_block, col_block = entry_r.shape[1:]
    levels = lax.dynamic_slice_in_dim(state_energies[0], row_index * states, states)
    bounds = lax.dynamic_slice_in_dim(radii_table, sec_index, 2)
    sector_width = (bounds[1] - bounds[0]).astype(jnp.float32)
    contraction = (((1,), (1,)), ((), ()))
    zeros = jnp.zeros((channels, channels), jnp.float32)
    sums = []
    for period in range(TICKS):
        energy = plan[0, period].astype(jnp.float32) / ENERGIES
        weight = 8.0 / (sector_width * (levels - energy))
        scaled = (panels.astype(jnp.float32) * weight).astype(jnp.bfloat16)
        ll = lax.dot_general(scaled[0], panels[0], contraction, preferred_element_type=jnp.float32)
        lr = lax.dot_general(scaled[0], panels[1], contraction, preferred_element_type=jnp.float32)
        rr = lax.dot_general(scaled[1], panels[1], contraction, preferred_element_type=jnp.float32)
        if period == 0:
            tile = entry_r[0]
        else:
            tile = jnp.where(sec_index == 0, fresh_r[period - 1], 0.0)
        place = (col_index * row_block, row_index * col_block)
        tile = tile + lax.dynamic_slice(ll, place, (row_block, col_block))
        ll = lax.dynamic_update_slice(ll, tile, place)
        sums.append(lax.psum(jnp.stack([ll, lr, rr]), ("row", "col")))
    boundary = zeros
    results = []
    for period in range(TICKS):
        ll, lr, rr = sums[period]
        exit_full = eliminate(ll, lr, rr, boundary)
        results.append(
            lax.dynamic_slice(
                exit_full, (col_index * row_block, row_index * col_block), (row_block, col_block)
            )
        )
        if period + 1 < TICKS:
            boundary = shifted_2(exit_full, "sec", 1)
    return jnp.stack(results, 0)[:, None]


def solution(mesh):
    placed = (
        P("sec", None, "row", "col"),
        P("sec", "col"),
        P(),
        P("sec", None),
        P("sec", "col", "row"),
        P(None, "col", "row"),
    )
    return jax.shard_map(
        local, mesh=mesh, in_specs=placed, out_specs=P(None, "sec", "col", "row"), check_vma=False
    )
```

```python
import functools
import jax
import jax.numpy as jnp
from jax import lax
from jax.experimental import pallas as pl
from jax.experimental.pallas import tpu as pltpu
from jax.sharding import PartitionSpec as P

ENERGIES = 32
TICKS = 2
BLOCK = 128
SUB = 8
HIGHEST = lax.Precision.HIGHEST


MESH = pl.DeviceIdType.MESH


def worker(sector):
    return sector % 2


def span(block, blocks):
    if block < blocks // 2:
        return block, 0, (blocks - block) * BLOCK
    mate = blocks - 1 - block
    return mate, (blocks - mate) * BLOCK, (blocks - block) * BLOCK


def inverse_factor(block):
    size = block.shape[0]
    groups = size // SUB
    sub_rows = lax.broadcasted_iota(jnp.int32, (SUB, size), 0)
    lanes = lax.broadcasted_iota(jnp.int32, (SUB, size), 1)
    left = [block[SUB * g : SUB * (g + 1), :] for g in range(groups)]
    right = [jnp.where(lanes == sub_rows + SUB * g, 1.0, 0.0) for g in range(groups)]
    done = []
    for g in range(groups):
        base = SUB * g
        u, v = left[g], right[g]
        cols = [jnp.broadcast_to(u[:, base + q : base + q + 1], (SUB, size)) for q in range(SUB)]
        scale = jnp.zeros((SUB, size), jnp.float32)
        for p in range(SUB):
            pivot = cols[p][p : p + 1, :]
            scale = jnp.where(sub_rows == p, pivot, scale)
            if p + 1 < SUB:
                f = jnp.where(sub_rows > p, cols[p] / pivot, 0.0)
                u = u - f * u[p : p + 1, :]
                v = v - f * v[p : p + 1, :]
                for q in range(p + 1, SUB):
                    cols[q] = cols[q] - f * cols[q][p : p + 1, :]
        scale = lax.rsqrt(scale)
        u = u * scale
        v = v * scale
        done.append(v)
        if g + 1 < groups:
            turned = u.T
            for h in range(g + 1, groups):
                for q in range(SUB):
                    c = jnp.broadcast_to(turned[SUB * h : SUB * (h + 1), q : q + 1], (SUB, size))
                    left[h] = left[h] - c * u[q : q + 1, :]
                    right[h] = right[h] - c * v[q : q + 1, :]
    return jnp.concatenate(done, 0)


def gather_kernel(
    rows, cols, amp_ref, weight_ref, tile_ref, first_ref, second_ref,
    panels, weights, tiles, scaled, parts, arrived,
    amp_send, amp_recv, small_send, small_recv, sum_send, sum_recv, full_send, full_recv,
):
    row, col = lax.axis_index("row"), lax.axis_index("col")
    home = worker(lax.axis_index("sec"))
    chunk = weight_ref.shape[1]
    row_block = amp_ref.shape[1]
    tile_rows = tile_ref.shape[1]
    channels = panels.shape[1]
    blocks = 2 * channels // BLOCK
    at_home = col == home

    barrier = pltpu.get_barrier_semaphore()
    for r in range(rows):
        for c in range(cols):

            @pl.when((row != r) | (col != c))
            def _():
                pl.semaphore_signal(
                    barrier, inc=1, device_id={"row": r, "col": c}, device_id_type=MESH
                )

    pl.semaphore_wait(barrier, rows * cols - 1)

    my_rows = pl.ds(pl.multiple_of(row * row_block, row_block), row_block)
    my_states = pl.ds(pl.multiple_of(col * chunk, chunk), chunk)
    my_tile = pl.ds(pl.multiple_of(col * tile_rows, tile_rows), tile_rows)
    source = row * cols + col

    def amp_there(r):
        return pltpu.make_async_remote_copy(
            src_ref=amp_ref.at[:, :, pl.ds(r * chunk, chunk)],
            dst_ref=panels.at[:, my_rows, my_states],
            send_sem=amp_send.at[r],
            recv_sem=amp_recv.at[source],
            device_id={"row": r, "col": home},
            device_id_type=MESH,
        )

    def amp_here(r):
        return pltpu.make_async_copy(
            amp_ref.at[:, :, pl.ds(r * chunk, chunk)],
            panels.at[:, my_rows, my_states],
            amp_send.at[r],
        )

    def small_there(src, dst, i):
        return pltpu.make_async_remote_copy(
            src_ref=src,
            dst_ref=dst,
            send_sem=small_send.at[i],
            recv_sem=small_recv.at[i, col],
            device_id={"col": home},
            device_id_type=MESH,
        )

    smalls = [
        (weight_ref, weights.at[:, my_states]),
        (tile_ref, tiles.at[:, my_tile, :]),
    ]
    for i, (src, dst) in enumerate(smalls):

        @pl.when(at_home)
        def _():
            pltpu.make_async_copy(src, dst, small_send.at[i]).start()

        @pl.when(jnp.logical_not(at_home))
        def _():
            small_there(src, dst, i).start()

    for r in range(rows):
        here = at_home & (row == r)

        @pl.when(here)
        def _():
            amp_here(r).start()

        @pl.when(jnp.logical_not(here))
        def _():
            amp_there(r).start()

    for i, (src, dst) in enumerate(smalls):

        @pl.when(at_home)
        def _():
            pltpu.make_async_copy(src, dst, small_send.at[i]).wait()

        @pl.when(jnp.logical_not(at_home))
        def _():
            small_there(src, dst, i).wait_send()

    for r in range(rows):
        here = at_home & (row == r)

        @pl.when(here)
        def _():
            amp_here(r).wait()

        @pl.when(jnp.logical_not(here))
        def _():
            amp_there(r).wait_send()

    @pl.when(jnp.logical_not(at_home))
    def _():
        first_ref[...] = jnp.zeros_like(first_ref)
        second_ref[...] = jnp.zeros_like(second_ref)

    def sum_copy(period, d):
        other = lax.rem(row + d, rows)
        return pltpu.make_async_remote_copy(
            src_ref=parts.at[period, other],
            dst_ref=arrived.at[period, d - 1],
            send_sem=sum_send.at[period, d - 1],
            recv_sem=sum_recv.at[period, d - 1],
            device_id={"row": other},
            device_id_type=MESH,
        )

    def full_copy(d):
        other = lax.rem(row + d, rows)
        return pltpu.make_async_remote_copy(
            src_ref=first_ref.at[row],
            dst_ref=first_ref.at[row],
            send_sem=full_send.at[d - 1],
            recv_sem=full_recv.at[d - 1],
            device_id={"row": other},
            device_id_type=MESH,
        )

    def full_arrival(d):
        other = lax.rem(row + rows - d, rows)
        return pltpu.make_async_remote_copy(
            src_ref=first_ref.at[row],
            dst_ref=first_ref.at[other],
            send_sem=full_send.at[d - 1],
            recv_sem=full_recv.at[d - 1],
            device_id={"row": lax.rem(row + d, rows)},
            device_id_type=MESH,
        )

    def greens(period):
        weight = weights[period : period + 1, :]
        for side in range(2):
            scaled[side] = (panels[side].astype(jnp.float32) * weight).astype(jnp.bfloat16)
        contraction = (((1,), (1,)), ((), ()))
        for left, right, first_block, first_column in (
            (0, 0, 0, 0),
            (0, 1, 0, channels),
            (1, 1, channels // BLOCK, channels),
        ):
            for i in range(0, channels, 2 * BLOCK):
                begin = i if left == right else 0
                green = lax.dot_general(
                    scaled[left, i : i + 2 * BLOCK, :],
                    panels[right, begin:, :],
                    contraction,
                    preferred_element_type=jnp.float32,
                )
                for j in range(2):
                    block = first_block + i // BLOCK + j
                    pair, start, _ = span(block, blocks)
                    skip = j * BLOCK if left == right else 0
                    at = start + first_column + begin + skip - block * BLOCK
                    wide = channels - begin - skip
                    parts[period, pair, :, at : at + wide] = green[
                        j * BLOCK : (j + 1) * BLOCK, skip:
                    ]
        for r in range(rows):

            @pl.when(row == r)
            def _():
                for block in range(r + 1):
                    pair, start, _ = span(block, blocks)
                    at = start + (r - block) * BLOCK
                    parts[period, pair, :, at : at + BLOCK] += tiles[
                        period, block * BLOCK : (block + 1) * BLOCK, :
                    ]

    def total(period):
        out = parts[period, row]
        for d in range(1, rows):
            out = out + arrived[period, d - 1]
        return out

    @pl.when(at_home)
    def _():
        for c in range(cols):

            @pl.when(col != c)
            def _():
                for i in range(2):
                    dst = (
                        weights.at[:, pl.ds(c * chunk, chunk)],
                        tiles.at[:, pl.ds(c * tile_rows, tile_rows), :],
                    )[i]
                    pltpu.make_async_remote_copy(
                        src_ref=dst, dst_ref=dst, send_sem=small_send.at[i],
                        recv_sem=small_recv.at[i, c], device_id={"col": c}, device_id_type=MESH,
                    ).wait_recv()

            for r in range(rows):

                @pl.when((row != r) | (col != c))
                def _():
                    dst = panels.at[
                        :, pl.ds(r * row_block, row_block), pl.ds(c * chunk, chunk)
                    ]
                    pltpu.make_async_remote_copy(
                        src_ref=dst, dst_ref=dst, send_sem=amp_send.at[0],
                        recv_sem=amp_recv.at[r * cols + c], device_id={"row": r, "col": c},
                        device_id_type=MESH,
                    ).wait_recv()

        for period in range(TICKS):
            greens(period)
            for d in range(1, rows):
                sum_copy(period, d).start()
        for d in range(1, rows):
            sum_copy(0, d).wait()
        first_ref[row] = total(0)
        for d in range(1, rows):
            full_copy(d).start()
        for d in range(1, rows):
            sum_copy(1, d).wait()
        second_ref[...] = total(1)
        for d in range(1, rows):
            full_copy(d).wait_send()
            full_arrival(d).wait_recv()


def gather(panels, weight, tiles, rows, cols):
    _, row_block, states = panels.shape
    chunk = states // rows
    channels = rows * row_block
    pairs = channels // BLOCK
    width = (2 * pairs + 1) * BLOCK
    assert row_block == BLOCK
    vmem = pl.BlockSpec(memory_space=pltpu.VMEM)
    dma = pltpu.SemaphoreType.DMA
    return pl.pallas_call(
        functools.partial(gather_kernel, rows, cols),
        out_shape=(
            jax.ShapeDtypeStruct((pairs, BLOCK, width), jnp.float32),
            jax.ShapeDtypeStruct((BLOCK, width), jnp.float32),
        ),
        in_specs=[pl.BlockSpec(memory_space=pl.ANY), vmem, vmem],
        out_specs=(vmem, vmem),
        scratch_shapes=[
            pltpu.VMEM((2, channels, cols * chunk), jnp.bfloat16),
            pltpu.VMEM((weight.shape[0], cols * chunk), jnp.float32),
            pltpu.VMEM((TICKS, channels, BLOCK), jnp.float32),
            pltpu.VMEM((2, channels, cols * chunk), jnp.bfloat16),
            pltpu.VMEM((TICKS, pairs, BLOCK, width), jnp.float32),
            pltpu.VMEM((TICKS, rows - 1, BLOCK, width), jnp.float32),
            dma((rows,)),
            dma((rows * cols,)),
            dma((2,)),
            dma((2, cols)),
            dma((TICKS, rows - 1)),
            dma((TICKS, rows - 1)),
            dma((rows - 1,)),
            dma((rows - 1,)),
        ],
        compiler_params=pltpu.CompilerParams(
            collective_id=0, has_side_effects=True, vmem_limit_bytes=48 * 1024 * 1024
        ),
        name="gather",
    )(panels, weight, tiles)


def eliminate_kernel(sums_ref, entry_ref, out_ref, upper_ref, work):
    n = out_ref.shape[0]
    blocks = n // BLOCK
    for k in range(2 * blocks):
        pair, start, wide = span(k, 2 * blocks)
        work[k * BLOCK : (k + 1) * BLOCK, k * BLOCK :] = sums_ref[pair, :, start : start + wide]
        if k < blocks:
            pair, start, wide = span(k, blocks)
            work[k * BLOCK : (k + 1) * BLOCK, k * BLOCK : n] += entry_ref[
                pair, :, start : start + wide
            ]
    for k in range(blocks):
        lo, hi = k * BLOCK, (k + 1) * BLOCK
        factor = inverse_factor(work[lo:hi, lo:hi])
        solved = jnp.dot(
            factor, work[lo:hi, hi:], precision=HIGHEST, preferred_element_type=jnp.float32
        )
        for i in range(hi, 2 * n, BLOCK):
            work[i : i + BLOCK, i:] -= lax.dot_general(
                solved[:, i - hi : i - hi + BLOCK],
                solved[:, i - hi :],
                (((0,), (0,)), ((), ())),
                precision=HIGHEST,
                preferred_element_type=jnp.float32,
            )
    for i in range(blocks):
        pair, start, wide = span(i, blocks)
        upper_ref[pair, :, start : start + wide] = work[n + i * BLOCK : n + (i + 1) * BLOCK, n + i * BLOCK :]
        for j in range(i, blocks):
            tile = work[n + i * BLOCK : n + (i + 1) * BLOCK, n + j * BLOCK : n + (j + 1) * BLOCK]
            out_ref[i * BLOCK : (i + 1) * BLOCK, j * BLOCK : (j + 1) * BLOCK] = tile
            if j > i:
                out_ref[j * BLOCK : (j + 1) * BLOCK, i * BLOCK : (i + 1) * BLOCK] = tile.T


def eliminate(sums, entry):
    n = sums.shape[0] * BLOCK
    blocks = n // BLOCK
    vmem = pl.BlockSpec(memory_space=pltpu.VMEM)
    return pl.pallas_call(
        eliminate_kernel,
        out_shape=(
            jax.ShapeDtypeStruct((n, n), jnp.float32),
            jax.ShapeDtypeStruct((blocks // 2, BLOCK, (blocks + 1) * BLOCK), jnp.float32),
        ),
        in_specs=[vmem] * 2,
        out_specs=(vmem, vmem),
        scratch_shapes=[pltpu.VMEM((2 * n, 2 * n), jnp.float32)],
        compiler_params=pltpu.CompilerParams(vmem_limit_bytes=32 * 1024 * 1024),
        cost_estimate=pl.CostEstimate(
            flops=200 * n * n * n, bytes_accessed=20 * n * n, transcendentals=0
        ),
        name="eliminate",
    )(sums, entry)


def local(amplitudes, state_energies, radii_table, plan, entry_r, fresh_r):
    sec_index = lax.axis_index("sec")
    row_index = lax.axis_index("row")
    col_index = lax.axis_index("col")
    sectors, rows, cols = (lax.axis_size(axis) for axis in ("sec", "row", "col"))
    home = worker(sec_index)
    panels = amplitudes[0]
    chunk = panels.shape[2] // rows
    tile_rows, tile_columns = entry_r.shape[1:]
    levels = lax.dynamic_slice_in_dim(state_energies[0], row_index * chunk, chunk)
    bounds = lax.dynamic_slice_in_dim(radii_table, sec_index, 2)
    sector_width = (bounds[1] - bounds[0]).astype(jnp.float32)
    energies = plan[0].astype(jnp.float32) / ENERGIES
    weight = 8.0 / (sector_width * (levels[None, :] - energies[:, None]))
    weight = jnp.pad(weight, ((0, SUB - TICKS), (0, 0)))
    tiles = jnp.concatenate([entry_r, jnp.where(sec_index == 0, fresh_r, 0.0)], 0)
    first, second = gather(panels, weight, tiles, rows, cols)
    second = lax.all_gather(second, "row", axis=0, tiled=False)

    def tile_of(full, col):
        return lax.dynamic_slice(
            full, (col * tile_rows, row_index * tile_columns), (tile_rows, tile_columns)
        )

    def spread(full):
        tile = tile_of(full, col_index)
        for d in range(1, cols):
            route = [
                (s * cols + worker(s), s * cols + (worker(s) + d) % cols) for s in range(sectors)
            ]
            moved = lax.ppermute(tile_of(full, (home + d) % cols), ("sec", "col"), route)
            tile = jnp.where(col_index == (home + d) % cols, moved, tile)
        return tile

    channels = rows * tile_columns
    blocks = channels // BLOCK
    boundary = jnp.zeros((blocks // 2, BLOCK, (blocks + 1) * BLOCK), jnp.float32)
    results = []
    for period, sums in enumerate((first, second)):
        full, upper = eliminate(sums, boundary)
        results.append(spread(full))
        if period + 1 < TICKS:
            route = [
                (s * cols + worker(s), (s + 1) * cols + worker(s + 1)) for s in range(sectors - 1)
            ]
            boundary = lax.ppermute(upper, ("sec", "col"), route)
    return jnp.stack(results, 0)[:, None]


def solution(mesh):
    placed = (
        P("sec", None, "row", "col"),
        P("sec", "col"),
        P(),
        P("sec", None),
        P("sec", "col", "row"),
        P(None, "col", "row"),
    )
    return jax.shard_map(
        local, mesh=mesh, in_specs=placed, out_specs=P(None, "sec", "col", "row"), check_vma=False
    )
```

```python
import functools
import jax
import jax.numpy as jnp
from jax import lax
from jax.experimental import pallas as pl
from jax.experimental.pallas import tpu as pltpu
from jax.sharding import PartitionSpec as P

ENERGIES = 32
TICKS = 2
BLOCK = 128
SUB = 8
HIGHEST = lax.Precision.HIGHEST


MESH = pl.DeviceIdType.MESH


def worker(sector):
    return sector % 2


def span(block, blocks):
    if block < blocks // 2:
        return block, 0, (blocks - block) * BLOCK
    mate = blocks - 1 - block
    return mate, (blocks - mate) * BLOCK, (blocks - block) * BLOCK


def inverse_factor(block):
    size = block.shape[0]
    groups = size // SUB
    sub_rows = lax.broadcasted_iota(jnp.int32, (SUB, size), 0)
    left = block
    right = jnp.where(
        lax.broadcasted_iota(jnp.int32, (size, size), 0)
        == lax.broadcasted_iota(jnp.int32, (size, size), 1),
        1.0,
        0.0,
    )
    done = []
    for g in range(groups):
        base = SUB * g
        u, v = left[:SUB], right[:SUB]
        cols = [jnp.broadcast_to(u[:, base + q : base + q + 1], (SUB, size)) for q in range(SUB)]
        scale = jnp.zeros((SUB, size), jnp.float32)
        for p in range(SUB):
            pivot = cols[p][p : p + 1, :]
            scale = jnp.where(sub_rows == p, pivot, scale)
            if p + 1 < SUB:
                f = jnp.where(sub_rows > p, cols[p] / pivot, 0.0)
                u = u - f * u[p : p + 1, :]
                v = v - f * v[p : p + 1, :]
                for q in range(p + 1, SUB):
                    cols[q] = cols[q] - f * cols[q][p : p + 1, :]
        scale = lax.rsqrt(scale)
        u = u * scale
        v = v * scale
        done.append(v)
        if g + 1 < groups:
            turned = u.T[base + SUB :, :]
            left, right = left[SUB:], right[SUB:]
            for q in range(SUB):
                c = jnp.broadcast_to(turned[:, q : q + 1], turned.shape[:1] + (size,))
                left = left - c * u[q : q + 1, :]
                right = right - c * v[q : q + 1, :]
    return jnp.concatenate(done, 0)


def gather_kernel(
    rows, cols, sectors, amp_ref, weight_ref, tile_ref, out_ref,
    panels, weights, tiles, scaled, parts, arrived, work, factor_ref, full, upper, inbox,
    amp_send, amp_recv, small_send, small_recv, sum_send, sum_recv,
    tile_send, tile_recv, shift_send, shift_recv,
):
    row, col = lax.axis_index("row"), lax.axis_index("col")
    sec = lax.axis_index("sec")
    home = worker(sec)
    root = (rows - 1) // 2
    chunk = weight_ref.shape[1]
    row_block = amp_ref.shape[1]
    tile_rows = tile_ref.shape[1]
    channels = panels.shape[1]
    blocks = 2 * channels // BLOCK
    at_home = col == home
    at_root = at_home & (row == root)

    barrier = pltpu.get_barrier_semaphore()
    for r in range(rows):
        for c in range(cols):

            @pl.when((row != r) | (col != c))
            def _():
                pl.semaphore_signal(
                    barrier, inc=1, device_id={"row": r, "col": c}, device_id_type=MESH
                )

    for step in (-1, 1):

        @pl.when(at_root & (sec + step >= 0) & (sec + step < sectors))
        def _():
            pl.semaphore_signal(
                barrier,
                inc=1,
                device_id={"sec": sec + step, "col": worker(sec + step + 2)},
                device_id_type=MESH,
            )

    before = jnp.where(at_root & (sec > 0), 1, 0)
    after = jnp.where(at_root & (sec < sectors - 1), 1, 0)
    pl.semaphore_wait(barrier, rows * cols - 1 + before + after)

    my_rows = pl.ds(pl.multiple_of(row * row_block, row_block), row_block)
    my_states = pl.ds(pl.multiple_of(col * chunk, chunk), chunk)
    my_tile = pl.ds(pl.multiple_of(col * tile_rows, tile_rows), tile_rows)
    source = row * cols + col

    def amp_there(r):
        return pltpu.make_async_remote_copy(
            src_ref=amp_ref.at[:, :, pl.ds(r * chunk, chunk)],
            dst_ref=panels.at[:, my_rows, my_states],
            send_sem=amp_send.at[r],
            recv_sem=amp_recv.at[source],
            device_id={"row": r, "col": home},
            device_id_type=MESH,
        )

    def amp_here(r):
        return pltpu.make_async_copy(
            amp_ref.at[:, :, pl.ds(r * chunk, chunk)],
            panels.at[:, my_rows, my_states],
            amp_send.at[r],
        )

    def small_there(src, dst, i):
        return pltpu.make_async_remote_copy(
            src_ref=src,
            dst_ref=dst,
            send_sem=small_send.at[i],
            recv_sem=small_recv.at[i, col],
            device_id={"col": home},
            device_id_type=MESH,
        )

    smalls = [
        (weight_ref, weights.at[:, my_states]),
        (tile_ref, tiles.at[:, my_tile, :]),
    ]
    for i, (src, dst) in enumerate(smalls):

        @pl.when(at_home)
        def _():
            pltpu.make_async_copy(src, dst, small_send.at[i]).start()

        @pl.when(jnp.logical_not(at_home))
        def _():
            small_there(src, dst, i).start()

    for r in range(rows):
        here = at_home & (row == r)

        @pl.when(here)
        def _():
            amp_here(r).start()

        @pl.when(jnp.logical_not(here))
        def _():
            amp_there(r).start()

    for i, (src, dst) in enumerate(smalls):

        @pl.when(at_home)
        def _():
            pltpu.make_async_copy(src, dst, small_send.at[i]).wait()

        @pl.when(jnp.logical_not(at_home))
        def _():
            small_there(src, dst, i).wait_send()

    for r in range(rows):
        here = at_home & (row == r)

        @pl.when(here)
        def _():
            amp_here(r).wait()

        @pl.when(jnp.logical_not(here))
        def _():
            amp_there(r).wait_send()

    half = BLOCK // 2
    pieces = [(pair, h) for pair in range(blocks // 2) for h in range(2)]

    def piece_copy(period, i, side):
        pair, h = pieces[i]
        return pltpu.make_async_remote_copy(
            src_ref=parts.at[period, pair, pl.ds(h * half, half)],
            dst_ref=arrived.at[period, side, pair, pl.ds(h * half, half)],
            send_sem=sum_send.at[period, i],
            recv_sem=sum_recv.at[period, side, i],
            device_id={"row": row - 1 if side == 0 else row + 1},
            device_id_type=MESH,
        )

    def piece_arrival(period, i, side):
        pair, h = pieces[i]
        return pltpu.make_async_remote_copy(
            src_ref=parts.at[period, pair, pl.ds(h * half, half)],
            dst_ref=arrived.at[period, side, pair, pl.ds(h * half, half)],
            send_sem=sum_send.at[period, i],
            recv_sem=sum_recv.at[period, side, i],
            device_id={"row": row + 1 if side == 0 else row - 1},
            device_id_type=MESH,
        )

    def pass_on(period, side, inner):
        for i, (pair, h) in enumerate(pieces):
            at = slice(h * half, (h + 1) * half)

            @pl.when(inner)
            def _():
                piece_arrival(period, i, side).wait_recv()
                parts[period, pair, at, :] += arrived[period, side, pair, at, :]

            piece_copy(period, i, side).start()
        for i in range(len(pieces)):
            piece_copy(period, i, side).wait_send()

    def take_sums(period):
        for pair in range(blocks // 2):
            for h in range(2):
                i = 2 * pair + h
                if root < rows - 1:
                    piece_arrival(period, i, 0).wait_recv()
                if root > 0:
                    piece_arrival(period, i, 1).wait_recv()
            for block in (pair, blocks - 1 - pair):
                _, start, wide = span(block, blocks)
                total = parts[period, pair, :, start : start + wide]
                if root < rows - 1:
                    total = total + arrived[period, 0, pair, :, start : start + wide]
                if root > 0:
                    total = total + arrived[period, 1, pair, :, start : start + wide]
                work[block * BLOCK : (block + 1) * BLOCK, block * BLOCK :] = total

    half_blocks = blocks // 2

    def shift_copy(step):
        return pltpu.make_async_remote_copy(
            src_ref=upper,
            dst_ref=inbox,
            send_sem=shift_send,
            recv_sem=shift_recv,
            device_id={"sec": sec + step, "col": worker(sec + step + 2)},
            device_id_type=MESH,
        )

    def tile_copy(period, r, c):
        return pltpu.make_async_remote_copy(
            src_ref=full.at[period, pl.ds(c * tile_rows, tile_rows), pl.ds(r * row_block, row_block)],
            dst_ref=out_ref.at[period],
            send_sem=tile_send.at[period, r * cols + c],
            recv_sem=tile_recv.at[period],
            device_id={"row": r, "col": c},
            device_id_type=MESH,
        )

    def tile_here(period, c):
        return pltpu.make_async_copy(
            full.at[period, pl.ds(c * tile_rows, tile_rows), pl.ds(root * row_block, row_block)],
            out_ref.at[period],
            tile_send.at[period, root * cols + c],
        )

    def each_tile(period, there, here):
        for c in range(cols):
            for r in range(rows):
                if r == root:

                    @pl.when(col == c)
                    def _():
                        here(tile_here(period, c))

                    @pl.when(col != c)
                    def _():
                        there(tile_copy(period, r, c))

                else:
                    there(tile_copy(period, r, c))

    def eliminate(period):
        def step(k, carry):
            lo = pl.multiple_of(k * BLOCK, BLOCK)
            factor_ref[...] = inverse_factor(work[pl.ds(lo, BLOCK), pl.ds(lo, BLOCK)])
            for j in range(half_blocks):

                @pl.when(k == j)
                def _():
                    hi = (j + 1) * BLOCK
                    solved = jnp.dot(
                        factor_ref[...],
                        work[j * BLOCK : hi, hi:],
                        precision=HIGHEST,
                        preferred_element_type=jnp.float32,
                    )
                    for i in range(hi, 2 * channels, BLOCK):
                        work[i : i + BLOCK, i:] -= lax.dot_general(
                            solved[:, i - hi : i - hi + BLOCK],
                            solved[:, i - hi :],
                            (((0,), (0,)), ((), ())),
                            precision=HIGHEST,
                            preferred_element_type=jnp.float32,
                        )

            return carry

        lax.fori_loop(0, half_blocks, step, 0)
        for i in range(half_blocks):
            lo = channels + i * BLOCK
            pair, start, wide = span(i, half_blocks)

            @pl.when(period == 0)
            def _():
                upper[pair, :, start : start + wide] = work[lo : lo + BLOCK, lo:]

            for j in range(i, half_blocks):
                at = channels + j * BLOCK
                tile = work[lo : lo + BLOCK, at : at + BLOCK]
                full[period, i * BLOCK : (i + 1) * BLOCK, j * BLOCK : (j + 1) * BLOCK] = tile
                if j > i:
                    full[period, j * BLOCK : (j + 1) * BLOCK, i * BLOCK : (i + 1) * BLOCK] = tile.T

    def greens(period):
        weight = weights[pl.ds(period, 1), :]
        for side in range(2):
            scaled[side] = (panels[side].astype(jnp.float32) * weight).astype(jnp.bfloat16)
        contraction = (((1,), (1,)), ((), ()))
        for left, right, first_block, first_column in (
            (0, 0, 0, 0),
            (0, 1, 0, channels),
            (1, 1, channels // BLOCK, channels),
        ):
            for i in range(0, channels, 2 * BLOCK):
                begin = i if left == right else 0
                green = lax.dot_general(
                    scaled[left, i : i + 2 * BLOCK, :],
                    panels[right, begin:, :],
                    contraction,
                    preferred_element_type=jnp.float32,
                )
                for j in range(2):
                    block = first_block + i // BLOCK + j
                    pair, start, _ = span(block, blocks)
                    skip = j * BLOCK if left == right else 0
                    at = start + first_column + begin + skip - block * BLOCK
                    wide = channels - begin - skip
                    parts[period, pair, :, at : at + wide] = green[
                        j * BLOCK : (j + 1) * BLOCK, skip:
                    ]
        for r in range(rows):

            @pl.when(row == r)
            def _():
                for block in range(r + 1):
                    pair, start, _ = span(block, blocks)
                    at = start + (r - block) * BLOCK
                    parts[period, pair, :, at : at + BLOCK] += tiles[
                        period, block * BLOCK : (block + 1) * BLOCK, :
                    ]

    @pl.when(at_home)
    def _():
        for c in range(cols):

            @pl.when(col != c)
            def _():
                for i in range(2):
                    dst = (
                        weights.at[:, pl.ds(c * chunk, chunk)],
                        tiles.at[:, pl.ds(c * tile_rows, tile_rows), :],
                    )[i]
                    pltpu.make_async_remote_copy(
                        src_ref=dst, dst_ref=dst, send_sem=small_send.at[i],
                        recv_sem=small_recv.at[i, c], device_id={"col": c}, device_id_type=MESH,
                    ).wait_recv()

            for r in range(rows):

                @pl.when((row != r) | (col != c))
                def _():
                    dst = panels.at[
                        :, pl.ds(r * row_block, row_block), pl.ds(c * chunk, chunk)
                    ]
                    pltpu.make_async_remote_copy(
                        src_ref=dst, dst_ref=dst, send_sem=amp_send.at[0],
                        recv_sem=amp_recv.at[r * cols + c], device_id={"row": r, "col": c},
                        device_id_type=MESH,
                    ).wait_recv()

        def tick(period, carry):
            greens(period)

            @pl.when(row > root)
            def _():
                pass_on(period, 0, row < rows - 1)

            @pl.when(row < root)
            def _():
                pass_on(period, 1, row > 0)

            @pl.when(row == root)
            def _():
                take_sums(period)

                @pl.when((period > 0) & (sec > 0))
                def _():
                    shift_copy(-1).wait_recv()
                    for k in range(half_blocks):
                        pair, start, wide = span(k, half_blocks)
                        work[k * BLOCK : (k + 1) * BLOCK, k * BLOCK : channels] += inbox[
                            pair, :, start : start + wide
                        ]

                eliminate(period)

                @pl.when((period == 0) & (sec < sectors - 1))
                def _():
                    shift_copy(1).start()

                each_tile(period, lambda copy: copy.start(), lambda copy: copy.start())

            return carry

        lax.fori_loop(0, TICKS, tick, 0)

    @pl.when(at_root)
    def _():
        @pl.when(sec < sectors - 1)
        def _():
            shift_copy(1).wait_send()

        for period in range(TICKS):
            each_tile(period, lambda copy: copy.wait_send(), lambda copy: copy.wait())

    @pl.when(jnp.logical_not(at_root))
    def _():
        for period in range(TICKS):
            pltpu.make_async_remote_copy(
                src_ref=out_ref.at[period],
                dst_ref=out_ref.at[period],
                send_sem=tile_send.at[period, 0],
                recv_sem=tile_recv.at[period],
                device_id={"row": root, "col": home},
                device_id_type=MESH,
            ).wait_recv()


def gather(panels, weight, tiles, rows, cols, sectors):
    _, row_block, states = panels.shape
    chunk = states // rows
    channels = rows * row_block
    pairs = channels // BLOCK
    width = (2 * pairs + 1) * BLOCK
    assert row_block == BLOCK and TICKS == 2
    vmem = pl.BlockSpec(memory_space=pltpu.VMEM)
    dma = pltpu.SemaphoreType.DMA
    f32, bf16 = jnp.float32, jnp.bfloat16
    packed = pltpu.VMEM((pairs // 2, BLOCK, (pairs + 1) * BLOCK), f32)
    return pl.pallas_call(
        functools.partial(gather_kernel, rows, cols, sectors),
        out_shape=jax.ShapeDtypeStruct(tiles.shape, f32),
        in_specs=[pl.BlockSpec(memory_space=pl.ANY), vmem, vmem],
        out_specs=vmem,
        scratch_shapes=[
            pltpu.VMEM((2, channels, cols * chunk), bf16),
            pltpu.VMEM((weight.shape[0], cols * chunk), f32),
            pltpu.VMEM((TICKS, channels, BLOCK), f32),
            pltpu.VMEM((2, channels, cols * chunk), bf16),
            pltpu.VMEM((TICKS, pairs, BLOCK, width), f32),
            pltpu.VMEM((TICKS, 2, pairs, BLOCK, width), f32),
            pltpu.VMEM((2 * channels, 2 * channels), f32),
            pltpu.VMEM((BLOCK, BLOCK), f32),
            pltpu.VMEM((TICKS, channels, channels), f32),
            packed,
            packed,
            dma((rows,)),
            dma((rows * cols,)),
            dma((2,)),
            dma((2, cols)),
            dma((TICKS, 2 * pairs)),
            dma((TICKS, 2, 2 * pairs)),
            dma((TICKS, rows * cols)),
            dma((TICKS,)),
            dma,
            dma,
        ],
        compiler_params=pltpu.CompilerParams(
            collective_id=0, has_side_effects=True, vmem_limit_bytes=52 * 1024 * 1024
        ),
        name="sectors",
    )(panels, weight, tiles)


def local(amplitudes, state_energies, radii_table, plan, entry_r, fresh_r):
    sec_index = lax.axis_index("sec")
    row_index = lax.axis_index("row")
    sectors, rows, cols = (lax.axis_size(axis) for axis in ("sec", "row", "col"))
    panels = amplitudes[0]
    chunk = panels.shape[2] // rows
    levels = lax.dynamic_slice_in_dim(state_energies[0], row_index * chunk, chunk)
    bounds = lax.dynamic_slice_in_dim(radii_table, sec_index, 2)
    sector_width = (bounds[1] - bounds[0]).astype(jnp.float32)
    energies = plan[0].astype(jnp.float32) / ENERGIES
    weight = 8.0 / (sector_width * (levels[None, :] - energies[:, None]))
    weight = jnp.pad(weight, ((0, SUB - TICKS), (0, 0)))
    tiles = jnp.concatenate([entry_r, jnp.where(sec_index == 0, fresh_r, 0.0)], 0)
    return gather(panels, weight, tiles, rows, cols, sectors)[:, None]


def solution(mesh):
    placed = (
        P("sec", None, "row", "col"),
        P("sec", "col"),
        P(),
        P("sec", None),
        P("sec", "col", "row"),
        P(None, "col", "row"),
    )
    return jax.shard_map(
        local, mesh=mesh, in_specs=placed, out_specs=P(None, "sec", "col", "row"), check_vma=False
    )
```

```python
import functools
import jax
import jax.numpy as jnp
from jax import lax
from jax.experimental import pallas as pl
from jax.experimental.pallas import tpu as pltpu
from jax.sharding import PartitionSpec as P

ENERGIES = 32
TICKS = 2
BLOCK = 128
SUB = 8
HIGHEST = lax.Precision.HIGHEST


MESH = pl.DeviceIdType.MESH


def worker(sector):
    return sector % 2


def span(block, blocks):
    if block < blocks // 2:
        return block, 0, (blocks - block) * BLOCK
    mate = blocks - 1 - block
    return mate, (blocks - mate) * BLOCK, (blocks - block) * BLOCK


def piece_list(blocks):
    pieces, of_block = [], []
    for block in range(blocks):
        pair, start, wide = span(block, blocks)
        mine = []
        for first in range(0, wide, 4 * BLOCK):
            mine.append(len(pieces))
            pieces.append((pair, start + first, min(4 * BLOCK, wide - first)))
        of_block.append(mine)
    return pieces, of_block


def inverse_factor(block):
    size = block.shape[0]
    groups = size // SUB
    sub_rows = lax.broadcasted_iota(jnp.int32, (SUB, size), 0)
    left = block
    right = jnp.where(
        lax.broadcasted_iota(jnp.int32, (size, size), 0)
        == lax.broadcasted_iota(jnp.int32, (size, size), 1),
        1.0,
        0.0,
    )
    done = []
    for g in range(groups):
        base = SUB * g
        u, v = left[:SUB], right[:SUB]
        cols = [jnp.broadcast_to(u[:, base + q : base + q + 1], (SUB, size)) for q in range(SUB)]
        scale = jnp.zeros((SUB, size), jnp.float32)
        for p in range(SUB):
            pivot = cols[p][p : p + 1, :]
            scale = jnp.where(sub_rows == p, pivot, scale)
            if p + 1 < SUB:
                f = jnp.where(sub_rows > p, cols[p] / pivot, 0.0)
                u = u - f * u[p : p + 1, :]
                v = v - f * v[p : p + 1, :]
                for q in range(p + 1, SUB):
                    cols[q] = cols[q] - f * cols[q][p : p + 1, :]
        scale = lax.rsqrt(scale)
        u = u * scale
        v = v * scale
        done.append(v)
        if g + 1 < groups:
            turned = u.T[base + SUB :, :]
            left, right = left[SUB:], right[SUB:]
            for q in range(SUB):
                c = jnp.broadcast_to(turned[:, q : q + 1], turned.shape[:1] + (size,))
                left = left - c * u[q : q + 1, :]
                right = right - c * v[q : q + 1, :]
    return jnp.concatenate(done, 0)


def gather_kernel(
    rows, cols, sectors, amp_ref, weight_ref, tile_ref, out_ref,
    panels, weights, tiles, scaled, parts, arrived, work, factor_ref, full, upper, inbox,
    amp_send, amp_recv, small_send, small_recv, sum_send, sum_recv,
    tile_send, tile_recv, shift_send, shift_recv,
):
    row, col = lax.axis_index("row"), lax.axis_index("col")
    sec = lax.axis_index("sec")
    home = worker(sec)
    root = (rows - 1) // 2
    chunk = weight_ref.shape[1]
    row_block = amp_ref.shape[1]
    tile_rows = tile_ref.shape[1]
    channels = panels.shape[1]
    blocks = 2 * channels // BLOCK
    at_home = col == home
    at_root = at_home & (row == root)

    barrier = pltpu.get_barrier_semaphore()
    for r in range(rows):
        for c in range(cols):

            @pl.when((row != r) | (col != c))
            def _():
                pl.semaphore_signal(
                    barrier, inc=1, device_id={"row": r, "col": c}, device_id_type=MESH
                )

    for step in (-1, 1):

        @pl.when(at_root & (sec + step >= 0) & (sec + step < sectors))
        def _():
            pl.semaphore_signal(
                barrier,
                inc=1,
                device_id={"sec": sec + step, "col": worker(sec + step + 2)},
                device_id_type=MESH,
            )

    before = jnp.where(at_root & (sec > 0), 1, 0)
    after = jnp.where(at_root & (sec < sectors - 1), 1, 0)
    pl.semaphore_wait(barrier, rows * cols - 1 + before + after)

    my_rows = pl.ds(pl.multiple_of(row * row_block, row_block), row_block)
    my_states = pl.ds(pl.multiple_of(col * chunk, chunk), chunk)
    my_tile = pl.ds(pl.multiple_of(col * tile_rows, tile_rows), tile_rows)
    source = row * cols + col

    def amp_there(r):
        return pltpu.make_async_remote_copy(
            src_ref=amp_ref.at[:, :, pl.ds(r * chunk, chunk)],
            dst_ref=panels.at[:, my_rows, my_states],
            send_sem=amp_send.at[r],
            recv_sem=amp_recv.at[source],
            device_id={"row": r, "col": home},
            device_id_type=MESH,
        )

    def amp_here(r):
        return pltpu.make_async_copy(
            amp_ref.at[:, :, pl.ds(r * chunk, chunk)],
            panels.at[:, my_rows, my_states],
            amp_send.at[r],
        )

    def small_there(src, dst, i):
        return pltpu.make_async_remote_copy(
            src_ref=src,
            dst_ref=dst,
            send_sem=small_send.at[i],
            recv_sem=small_recv.at[i, col],
            device_id={"col": home},
            device_id_type=MESH,
        )

    smalls = [
        (weight_ref, weights.at[:, my_states]),
        (tile_ref, tiles.at[:, my_tile, :]),
    ]
    for i, (src, dst) in enumerate(smalls):

        @pl.when(at_home)
        def _():
            pltpu.make_async_copy(src, dst, small_send.at[i]).start()

        @pl.when(jnp.logical_not(at_home))
        def _():
            small_there(src, dst, i).start()

    for r in range(rows):
        here = at_home & (row == r)

        @pl.when(here)
        def _():
            amp_here(r).start()

        @pl.when(jnp.logical_not(here))
        def _():
            amp_there(r).start()

    for i, (src, dst) in enumerate(smalls):

        @pl.when(at_home)
        def _():
            pltpu.make_async_copy(src, dst, small_send.at[i]).wait()

        @pl.when(jnp.logical_not(at_home))
        def _():
            small_there(src, dst, i).wait_send()

    for r in range(rows):
        here = at_home & (row == r)

        @pl.when(here)
        def _():
            amp_here(r).wait()

        @pl.when(jnp.logical_not(here))
        def _():
            amp_there(r).wait_send()

    pieces, of_block = piece_list(blocks)

    def piece_copy(period, i, side):
        pair, first, wide = pieces[i]
        return pltpu.make_async_remote_copy(
            src_ref=parts.at[period, pair, :, pl.ds(first, wide)],
            dst_ref=arrived.at[period, side, pair, :, pl.ds(first, wide)],
            send_sem=sum_send.at[period, i],
            recv_sem=sum_recv.at[period, side, i],
            device_id={"row": row - 1 if side == 0 else row + 1},
            device_id_type=MESH,
        )

    def piece_arrival(period, i, side):
        pair, first, wide = pieces[i]
        return pltpu.make_async_remote_copy(
            src_ref=parts.at[period, pair, :, pl.ds(first, wide)],
            dst_ref=arrived.at[period, side, pair, :, pl.ds(first, wide)],
            send_sem=sum_send.at[period, i],
            recv_sem=sum_recv.at[period, side, i],
            device_id={"row": row + 1 if side == 0 else row - 1},
            device_id_type=MESH,
        )

    def pass_on(period, side, inner):
        for i, (pair, first, wide) in enumerate(pieces):
            at = slice(first, first + wide)

            @pl.when(inner)
            def _():
                piece_arrival(period, i, side).wait_recv()
                parts[period, pair, :, at] += arrived[period, side, pair, :, at]

            piece_copy(period, i, side).start()
        for i in range(len(pieces)):
            piece_copy(period, i, side).wait_send()

    def take_sums(period, block):
        for i in of_block[block]:
            pair, first, wide = pieces[i]
            total = parts[period, pair, :, first : first + wide]
            if root < rows - 1:
                piece_arrival(period, i, 0).wait_recv()
                total = total + arrived[period, 0, pair, :, first : first + wide]
            if root > 0:
                piece_arrival(period, i, 1).wait_recv()
                total = total + arrived[period, 1, pair, :, first : first + wide]
            at = block * BLOCK + first - span(block, blocks)[1]
            work[block * BLOCK : (block + 1) * BLOCK, at : at + wide] += total

    half_blocks = blocks // 2

    def shift_copy(k, step):
        pair, start, wide = span(k, half_blocks)
        return pltpu.make_async_remote_copy(
            src_ref=upper.at[pair, :, pl.ds(start, wide)],
            dst_ref=inbox.at[pair, :, pl.ds(start, wide)],
            send_sem=shift_send.at[k],
            recv_sem=shift_recv.at[k],
            device_id={"sec": sec + step, "col": worker(sec + step + 2)},
            device_id_type=MESH,
        )

    def tile_copy(period, r, c):
        return pltpu.make_async_remote_copy(
            src_ref=full.at[period, pl.ds(c * tile_rows, tile_rows), pl.ds(r * row_block, row_block)],
            dst_ref=out_ref.at[period],
            send_sem=tile_send.at[period, r * cols + c],
            recv_sem=tile_recv.at[period],
            device_id={"row": r, "col": c},
            device_id_type=MESH,
        )

    def tile_here(period, c):
        return pltpu.make_async_copy(
            full.at[period, pl.ds(c * tile_rows, tile_rows), pl.ds(root * row_block, row_block)],
            out_ref.at[period],
            tile_send.at[period, root * cols + c],
        )

    def each_tile(period, there, here):
        for c in range(cols):
            for r in range(rows):
                if r == root:

                    @pl.when(col == c)
                    def _():
                        here(tile_here(period, c))

                    @pl.when(col != c)
                    def _():
                        there(tile_copy(period, r, c))

                else:
                    there(tile_copy(period, r, c))

    def eliminate(period):
        for block in range(blocks):
            wide = (blocks - block) * BLOCK
            work[block * BLOCK : (block + 1) * BLOCK, block * BLOCK :] = jnp.zeros(
                (BLOCK, wide), jnp.float32
            )

        def step(k, carry):
            for j in range(half_blocks):

                @pl.when(k == j)
                def _():
                    take_sums(period, j)

                @pl.when((k == j) & (period > 0) & (sec > 0))
                def _():
                    shift_copy(j, -1).wait_recv()
                    pair, start, wide = span(j, half_blocks)
                    work[j * BLOCK : (j + 1) * BLOCK, j * BLOCK : channels] += inbox[
                        pair, :, start : start + wide
                    ]

            lo = pl.multiple_of(k * BLOCK, BLOCK)
            factor_ref[...] = inverse_factor(work[pl.ds(lo, BLOCK), pl.ds(lo, BLOCK)])
            for j in range(half_blocks):

                @pl.when(k == j)
                def _():
                    hi = (j + 1) * BLOCK
                    solved = jnp.dot(
                        factor_ref[...],
                        work[j * BLOCK : hi, hi:],
                        precision=HIGHEST,
                        preferred_element_type=jnp.float32,
                    )
                    for i in range(hi, 2 * channels, BLOCK):
                        work[i : i + BLOCK, i:] -= lax.dot_general(
                            solved[:, i - hi : i - hi + BLOCK],
                            solved[:, i - hi :],
                            (((0,), (0,)), ((), ())),
                            precision=HIGHEST,
                            preferred_element_type=jnp.float32,
                        )

            return carry

        lax.fori_loop(0, half_blocks, step, 0)
        for i in range(half_blocks):
            take_sums(period, half_blocks + i)
            lo = channels + i * BLOCK
            pair, start, wide = span(i, half_blocks)

            @pl.when(period == 0)
            def _():
                upper[pair, :, start : start + wide] = work[lo : lo + BLOCK, lo:]

            @pl.when((period == 0) & (sec < sectors - 1))
            def _():
                shift_copy(i, 1).start()

            for j in range(i, half_blocks):
                at = channels + j * BLOCK
                tile = work[lo : lo + BLOCK, at : at + BLOCK]
                full[period, i * BLOCK : (i + 1) * BLOCK, j * BLOCK : (j + 1) * BLOCK] = tile
                if j > i:
                    full[period, j * BLOCK : (j + 1) * BLOCK, i * BLOCK : (i + 1) * BLOCK] = tile.T

    def greens(period):
        weight = weights[pl.ds(period, 1), :]
        for side in range(2):
            scaled[side] = (panels[side].astype(jnp.float32) * weight).astype(jnp.bfloat16)
        contraction = (((1,), (1,)), ((), ()))
        for left, right, first_block, first_column in (
            (0, 0, 0, 0),
            (0, 1, 0, channels),
            (1, 1, channels // BLOCK, channels),
        ):
            for i in range(0, channels, 2 * BLOCK):
                begin = i if left == right else 0
                green = lax.dot_general(
                    scaled[left, i : i + 2 * BLOCK, :],
                    panels[right, begin:, :],
                    contraction,
                    preferred_element_type=jnp.float32,
                )
                for j in range(2):
                    block = first_block + i // BLOCK + j
                    pair, start, _ = span(block, blocks)
                    skip = j * BLOCK if left == right else 0
                    at = start + first_column + begin + skip - block * BLOCK
                    wide = channels - begin - skip
                    parts[period, pair, :, at : at + wide] = green[
                        j * BLOCK : (j + 1) * BLOCK, skip:
                    ]
        for r in range(rows):

            @pl.when(row == r)
            def _():
                for block in range(r + 1):
                    pair, start, _ = span(block, blocks)
                    at = start + (r - block) * BLOCK
                    parts[period, pair, :, at : at + BLOCK] += tiles[
                        period, block * BLOCK : (block + 1) * BLOCK, :
                    ]

    @pl.when(at_home)
    def _():
        for c in range(cols):

            @pl.when(col != c)
            def _():
                for i in range(2):
                    dst = (
                        weights.at[:, pl.ds(c * chunk, chunk)],
                        tiles.at[:, pl.ds(c * tile_rows, tile_rows), :],
                    )[i]
                    pltpu.make_async_remote_copy(
                        src_ref=dst, dst_ref=dst, send_sem=small_send.at[i],
                        recv_sem=small_recv.at[i, c], device_id={"col": c}, device_id_type=MESH,
                    ).wait_recv()

            for r in range(rows):

                @pl.when((row != r) | (col != c))
                def _():
                    dst = panels.at[
                        :, pl.ds(r * row_block, row_block), pl.ds(c * chunk, chunk)
                    ]
                    pltpu.make_async_remote_copy(
                        src_ref=dst, dst_ref=dst, send_sem=amp_send.at[0],
                        recv_sem=amp_recv.at[r * cols + c], device_id={"row": r, "col": c},
                        device_id_type=MESH,
                    ).wait_recv()

        def own_greens(period, carry):
            greens(period)
            return carry

        @pl.when(row == root)
        def _():
            lax.fori_loop(0, TICKS, own_greens, 0)

        def tick(period, carry):
            @pl.when(row != root)
            def _():
                greens(period)

            @pl.when(row > root)
            def _():
                pass_on(period, 0, row < rows - 1)

            @pl.when(row < root)
            def _():
                pass_on(period, 1, row > 0)

            @pl.when(row == root)
            def _():
                eliminate(period)
                each_tile(period, lambda copy: copy.start(), lambda copy: copy.start())

            return carry

        lax.fori_loop(0, TICKS, tick, 0)

    @pl.when(at_root)
    def _():
        @pl.when(sec < sectors - 1)
        def _():
            for k in range(half_blocks):
                shift_copy(k, 1).wait_send()

        for period in range(TICKS):
            each_tile(period, lambda copy: copy.wait_send(), lambda copy: copy.wait())

    @pl.when(jnp.logical_not(at_root))
    def _():
        for period in range(TICKS):
            pltpu.make_async_remote_copy(
                src_ref=out_ref.at[period],
                dst_ref=out_ref.at[period],
                send_sem=tile_send.at[period, 0],
                recv_sem=tile_recv.at[period],
                device_id={"row": root, "col": home},
                device_id_type=MESH,
            ).wait_recv()


def gather(panels, weight, tiles, rows, cols, sectors):
    _, row_block, states = panels.shape
    chunk = states // rows
    channels = rows * row_block
    pairs = channels // BLOCK
    width = (2 * pairs + 1) * BLOCK
    pieces = len(piece_list(2 * pairs)[0])
    assert row_block == BLOCK and TICKS == 2
    vmem = pl.BlockSpec(memory_space=pltpu.VMEM)
    dma = pltpu.SemaphoreType.DMA
    f32, bf16 = jnp.float32, jnp.bfloat16
    packed = pltpu.VMEM((pairs // 2, BLOCK, (pairs + 1) * BLOCK), f32)
    return pl.pallas_call(
        functools.partial(gather_kernel, rows, cols, sectors),
        out_shape=jax.ShapeDtypeStruct(tiles.shape, f32),
        in_specs=[pl.BlockSpec(memory_space=pl.ANY), vmem, vmem],
        out_specs=vmem,
        scratch_shapes=[
            pltpu.VMEM((2, channels, cols * chunk), bf16),
            pltpu.VMEM((weight.shape[0], cols * chunk), f32),
            pltpu.VMEM((TICKS, channels, BLOCK), f32),
            pltpu.VMEM((2, channels, cols * chunk), bf16),
            pltpu.VMEM((TICKS, pairs, BLOCK, width), f32),
            pltpu.VMEM((TICKS, 2, pairs, BLOCK, width), f32),
            pltpu.VMEM((2 * channels, 2 * channels), f32),
            pltpu.VMEM((BLOCK, BLOCK), f32),
            pltpu.VMEM((TICKS, channels, channels), f32),
            packed,
            packed,
            dma((rows,)),
            dma((rows * cols,)),
            dma((2,)),
            dma((2, cols)),
            dma((TICKS, pieces)),
            dma((TICKS, 2, pieces)),
            dma((TICKS, rows * cols)),
            dma((TICKS,)),
            dma((pairs,)),
            dma((pairs,)),
        ],
        compiler_params=pltpu.CompilerParams(
            collective_id=0, has_side_effects=True, vmem_limit_bytes=52 * 1024 * 1024
        ),
        name="sectors",
    )(panels, weight, tiles)


def local(amplitudes, state_energies, radii_table, plan, entry_r, fresh_r):
    sec_index = lax.axis_index("sec")
    row_index = lax.axis_index("row")
    sectors, rows, cols = (lax.axis_size(axis) for axis in ("sec", "row", "col"))
    panels = amplitudes[0]
    chunk = panels.shape[2] // rows
    levels = lax.dynamic_slice_in_dim(state_energies[0], row_index * chunk, chunk)
    bounds = lax.dynamic_slice_in_dim(radii_table, sec_index, 2)
    sector_width = (bounds[1] - bounds[0]).astype(jnp.float32)
    energies = plan[0].astype(jnp.float32) / ENERGIES
    weight = 8.0 / (sector_width * (levels[None, :] - energies[:, None]))
    weight = jnp.pad(weight, ((0, SUB - TICKS), (0, 0)))
    tiles = jnp.concatenate([entry_r, jnp.where(sec_index == 0, fresh_r, 0.0)], 0)
    return gather(panels, weight, tiles, rows, cols, sectors)[:, None]


def solution(mesh):
    placed = (
        P("sec", None, "row", "col"),
        P("sec", "col"),
        P(),
        P("sec", None),
        P("sec", "col", "row"),
        P(None, "col", "row"),
    )
    return jax.shard_map(
        local, mesh=mesh, in_specs=placed, out_specs=P(None, "sec", "col", "row"), check_vma=False
    )
```

```python
import functools
import jax
import jax.numpy as jnp
from jax import lax
from jax.experimental import pallas as pl
from jax.experimental.pallas import tpu as pltpu
from jax.sharding import PartitionSpec as P

ENERGIES = 32
TICKS = 2
BLOCK = 128
SUB = 8
HIGHEST = lax.Precision.HIGHEST


MESH = pl.DeviceIdType.MESH


def worker(sector):
    return sector % 2


def span(block, blocks):
    if block < blocks // 2:
        return block, 0, (blocks - block) * BLOCK
    mate = blocks - 1 - block
    return mate, (blocks - mate) * BLOCK, (blocks - block) * BLOCK


def piece_list(blocks):
    pieces, of_block = [], []
    for block in range(blocks):
        pair, start, wide = span(block, blocks)
        mine = []
        for first in range(0, wide, 4 * BLOCK):
            mine.append(len(pieces))
            pieces.append((pair, start + first, min(4 * BLOCK, wide - first)))
        of_block.append(mine)
    return pieces, of_block


def inverse_factor(block):
    size = block.shape[0]
    groups = size // SUB
    sub_rows = lax.broadcasted_iota(jnp.int32, (SUB, size), 0)
    left = block
    right = jnp.where(
        lax.broadcasted_iota(jnp.int32, (size, size), 0)
        == lax.broadcasted_iota(jnp.int32, (size, size), 1),
        1.0,
        0.0,
    )
    done = []
    for g in range(groups):
        base = SUB * g
        u, v = left[:SUB], right[:SUB]
        cols = [jnp.broadcast_to(u[:, base + q : base + q + 1], (SUB, size)) for q in range(SUB)]
        scale = jnp.zeros((SUB, size), jnp.float32)
        for p in range(SUB):
            root = lax.rsqrt(cols[p][p : p + 1, :])
            scale = jnp.where(sub_rows == p, root, scale)
            if p + 1 < SUB:
                f = jnp.where(sub_rows > p, cols[p], 0.0) * (root * root)
                u = u - f * u[p : p + 1, :]
                v = v - f * v[p : p + 1, :]
                for q in range(p + 1, SUB):
                    cols[q] = cols[q] - f * cols[q][p : p + 1, :]
        u = u * scale
        v = v * scale
        done.append(v)
        if g + 1 < groups:
            turned = u.T[base + SUB :, :]
            left, right = left[SUB:], right[SUB:]
            for q in range(SUB):
                c = jnp.broadcast_to(turned[:, q : q + 1], turned.shape[:1] + (size,))
                left = left - c * u[q : q + 1, :]
                right = right - c * v[q : q + 1, :]
    return jnp.concatenate(done, 0)


def gather_kernel(
    rows, cols, sectors, amp_ref, weight_ref, tile_ref, out_ref,
    panels, weights, tiles, scaled, parts, arrived, work, factor_ref, full, upper, inbox,
    amp_send, amp_recv, small_send, small_recv, sum_send, sum_recv,
    tile_send, tile_recv, shift_send, shift_recv,
):
    row, col = lax.axis_index("row"), lax.axis_index("col")
    sec = lax.axis_index("sec")
    home = worker(sec)
    root = (rows - 1) // 2
    chunk = weight_ref.shape[1]
    row_block = amp_ref.shape[1]
    tile_rows = tile_ref.shape[1]
    channels = panels.shape[1]
    blocks = 2 * channels // BLOCK
    at_home = col == home
    at_root = at_home & (row == root)

    barrier = pltpu.get_barrier_semaphore()
    for r in range(rows):
        for c in range(cols):

            @pl.when((row != r) | (col != c))
            def _():
                pl.semaphore_signal(
                    barrier, inc=1, device_id={"row": r, "col": c}, device_id_type=MESH
                )

    for step in (-1, 1):

        @pl.when(at_root & (sec + step >= 0) & (sec + step < sectors))
        def _():
            pl.semaphore_signal(
                barrier,
                inc=1,
                device_id={"sec": sec + step, "col": worker(sec + step + 2)},
                device_id_type=MESH,
            )

    before = jnp.where(at_root & (sec > 0), 1, 0)
    after = jnp.where(at_root & (sec < sectors - 1), 1, 0)
    pl.semaphore_wait(barrier, rows * cols - 1 + before + after)

    my_rows = pl.ds(pl.multiple_of(row * row_block, row_block), row_block)
    my_states = pl.ds(pl.multiple_of(col * chunk, chunk), chunk)
    my_tile = pl.ds(pl.multiple_of(col * tile_rows, tile_rows), tile_rows)
    source = row * cols + col

    def amp_there(r):
        return pltpu.make_async_remote_copy(
            src_ref=amp_ref.at[:, :, pl.ds(r * chunk, chunk)],
            dst_ref=panels.at[:, my_rows, my_states],
            send_sem=amp_send.at[r],
            recv_sem=amp_recv.at[source],
            device_id={"row": r, "col": home},
            device_id_type=MESH,
        )

    def amp_here(r):
        return pltpu.make_async_copy(
            amp_ref.at[:, :, pl.ds(r * chunk, chunk)],
            panels.at[:, my_rows, my_states],
            amp_send.at[r],
        )

    def small_there(src, dst, i):
        return pltpu.make_async_remote_copy(
            src_ref=src,
            dst_ref=dst,
            send_sem=small_send.at[i],
            recv_sem=small_recv.at[i, col],
            device_id={"col": home},
            device_id_type=MESH,
        )

    smalls = [
        (weight_ref, weights.at[:, my_states]),
        (tile_ref, tiles.at[:, my_tile, :]),
    ]
    for i, (src, dst) in enumerate(smalls):

        @pl.when(at_home)
        def _():
            pltpu.make_async_copy(src, dst, small_send.at[i]).start()

        @pl.when(jnp.logical_not(at_home))
        def _():
            small_there(src, dst, i).start()

    for r in range(rows):
        here = at_home & (row == r)

        @pl.when(here)
        def _():
            amp_here(r).start()

        @pl.when(jnp.logical_not(here))
        def _():
            amp_there(r).start()

    for i, (src, dst) in enumerate(smalls):

        @pl.when(at_home)
        def _():
            pltpu.make_async_copy(src, dst, small_send.at[i]).wait()

        @pl.when(jnp.logical_not(at_home))
        def _():
            small_there(src, dst, i).wait_send()

    for r in range(rows):
        here = at_home & (row == r)

        @pl.when(here)
        def _():
            amp_here(r).wait()

        @pl.when(jnp.logical_not(here))
        def _():
            amp_there(r).wait_send()

    pieces, of_block = piece_list(blocks)

    def piece_copy(period, i, side):
        pair, first, wide = pieces[i]
        return pltpu.make_async_remote_copy(
            src_ref=parts.at[period, pair, :, pl.ds(first, wide)],
            dst_ref=arrived.at[period, side, pair, :, pl.ds(first, wide)],
            send_sem=sum_send.at[period, i],
            recv_sem=sum_recv.at[period, side, i],
            device_id={"row": row - 1 if side == 0 else row + 1},
            device_id_type=MESH,
        )

    def piece_arrival(period, i, side):
        pair, first, wide = pieces[i]
        return pltpu.make_async_remote_copy(
            src_ref=parts.at[period, pair, :, pl.ds(first, wide)],
            dst_ref=arrived.at[period, side, pair, :, pl.ds(first, wide)],
            send_sem=sum_send.at[period, i],
            recv_sem=sum_recv.at[period, side, i],
            device_id={"row": row + 1 if side == 0 else row - 1},
            device_id_type=MESH,
        )

    def pass_on(period, side, inner):
        for i, (pair, first, wide) in enumerate(pieces):
            at = slice(first, first + wide)

            @pl.when(inner)
            def _():
                piece_arrival(period, i, side).wait_recv()
                parts[period, pair, :, at] += arrived[period, side, pair, :, at]

            piece_copy(period, i, side).start()
        for i in range(len(pieces)):
            piece_copy(period, i, side).wait_send()

    def take_sums(period, block):
        for i in of_block[block]:
            pair, first, wide = pieces[i]
            total = parts[period, pair, :, first : first + wide]
            if root < rows - 1:
                piece_arrival(period, i, 0).wait_recv()
                total = total + arrived[period, 0, pair, :, first : first + wide]
            if root > 0:
                piece_arrival(period, i, 1).wait_recv()
                total = total + arrived[period, 1, pair, :, first : first + wide]
            at = block * BLOCK + first - span(block, blocks)[1]
            work[block * BLOCK : (block + 1) * BLOCK, at : at + wide] += total

    half_blocks = blocks // 2

    def shift_copy(k, step):
        pair, start, wide = span(k, half_blocks)
        return pltpu.make_async_remote_copy(
            src_ref=upper.at[pair, :, pl.ds(start, wide)],
            dst_ref=inbox.at[pair, :, pl.ds(start, wide)],
            send_sem=shift_send.at[k],
            recv_sem=shift_recv.at[k],
            device_id={"sec": sec + step, "col": worker(sec + step + 2)},
            device_id_type=MESH,
        )

    def tile_copy(period, r, c):
        return pltpu.make_async_remote_copy(
            src_ref=full.at[period, pl.ds(c * tile_rows, tile_rows), pl.ds(r * row_block, row_block)],
            dst_ref=out_ref.at[period],
            send_sem=tile_send.at[period, r * cols + c],
            recv_sem=tile_recv.at[period],
            device_id={"row": r, "col": c},
            device_id_type=MESH,
        )

    def tile_here(period, c):
        return pltpu.make_async_copy(
            full.at[period, pl.ds(c * tile_rows, tile_rows), pl.ds(root * row_block, row_block)],
            out_ref.at[period],
            tile_send.at[period, root * cols + c],
        )

    def each_tile(period, there, here):
        for c in range(cols):
            for r in range(rows):
                if r == root:

                    @pl.when(col == c)
                    def _():
                        here(tile_here(period, c))

                    @pl.when(col != c)
                    def _():
                        there(tile_copy(period, r, c))

                else:
                    there(tile_copy(period, r, c))

    def eliminate(period):
        for block in range(blocks):
            wide = (blocks - block) * BLOCK
            work[block * BLOCK : (block + 1) * BLOCK, block * BLOCK :] = jnp.zeros(
                (BLOCK, wide), jnp.float32
            )

        def step(k, carry):
            for j in range(half_blocks):

                @pl.when(k == j)
                def _():
                    take_sums(period, j)

                @pl.when((k == j) & (period > 0) & (sec > 0))
                def _():
                    shift_copy(j, -1).wait_recv()
                    pair, start, wide = span(j, half_blocks)
                    work[j * BLOCK : (j + 1) * BLOCK, j * BLOCK : channels] += inbox[
                        pair, :, start : start + wide
                    ]

            lo = pl.multiple_of(k * BLOCK, BLOCK)
            factor_ref[...] = inverse_factor(work[pl.ds(lo, BLOCK), pl.ds(lo, BLOCK)])
            for j in range(half_blocks):

                @pl.when(k == j)
                def _():
                    hi = (j + 1) * BLOCK
                    solved = jnp.dot(
                        factor_ref[...],
                        work[j * BLOCK : hi, hi:],
                        precision=HIGHEST,
                        preferred_element_type=jnp.float32,
                    )
                    for i in range(hi, 2 * channels, BLOCK):
                        work[i : i + BLOCK, i:] -= lax.dot_general(
                            solved[:, i - hi : i - hi + BLOCK],
                            solved[:, i - hi :],
                            (((0,), (0,)), ((), ())),
                            precision=HIGHEST,
                            preferred_element_type=jnp.float32,
                        )

            return carry

        lax.fori_loop(0, half_blocks, step, 0)
        for i in range(half_blocks):
            take_sums(period, half_blocks + i)
            lo = channels + i * BLOCK
            pair, start, wide = span(i, half_blocks)

            @pl.when(period == 0)
            def _():
                upper[pair, :, start : start + wide] = work[lo : lo + BLOCK, lo:]

            @pl.when((period == 0) & (sec < sectors - 1))
            def _():
                shift_copy(i, 1).start()

            for j in range(i, half_blocks):
                at = channels + j * BLOCK
                tile = work[lo : lo + BLOCK, at : at + BLOCK]
                full[period, i * BLOCK : (i + 1) * BLOCK, j * BLOCK : (j + 1) * BLOCK] = tile
                if j > i:
                    full[period, j * BLOCK : (j + 1) * BLOCK, i * BLOCK : (i + 1) * BLOCK] = tile.T

    def greens(period):
        weight = weights[pl.ds(period, 1), :]
        for side in range(2):
            scaled[side] = (panels[side].astype(jnp.float32) * weight).astype(jnp.bfloat16)
        contraction = (((1,), (1,)), ((), ()))
        for left, right, first_block, first_column in (
            (0, 0, 0, 0),
            (0, 1, 0, channels),
            (1, 1, channels // BLOCK, channels),
        ):
            for i in range(0, channels, 2 * BLOCK):
                begin = i if left == right else 0
                green = lax.dot_general(
                    scaled[left, i : i + 2 * BLOCK, :],
                    panels[right, begin:, :],
                    contraction,
                    preferred_element_type=jnp.float32,
                )
                for j in range(2):
                    block = first_block + i // BLOCK + j
                    pair, start, _ = span(block, blocks)
                    skip = j * BLOCK if left == right else 0
                    at = start + first_column + begin + skip - block * BLOCK
                    wide = channels - begin - skip
                    parts[period, pair, :, at : at + wide] = green[
                        j * BLOCK : (j + 1) * BLOCK, skip:
                    ]
        for r in range(rows):

            @pl.when(row == r)
            def _():
                for block in range(r + 1):
                    pair, start, _ = span(block, blocks)
                    at = start + (r - block) * BLOCK
                    parts[period, pair, :, at : at + BLOCK] += tiles[
                        period, block * BLOCK : (block + 1) * BLOCK, :
                    ]

    @pl.when(at_home)
    def _():
        for c in range(cols):

            @pl.when(col != c)
            def _():
                for i in range(2):
                    dst = (
                        weights.at[:, pl.ds(c * chunk, chunk)],
                        tiles.at[:, pl.ds(c * tile_rows, tile_rows), :],
                    )[i]
                    pltpu.make_async_remote_copy(
                        src_ref=dst, dst_ref=dst, send_sem=small_send.at[i],
                        recv_sem=small_recv.at[i, c], device_id={"col": c}, device_id_type=MESH,
                    ).wait_recv()

            for r in range(rows):

                @pl.when((row != r) | (col != c))
                def _():
                    dst = panels.at[
                        :, pl.ds(r * row_block, row_block), pl.ds(c * chunk, chunk)
                    ]
                    pltpu.make_async_remote_copy(
                        src_ref=dst, dst_ref=dst, send_sem=amp_send.at[0],
                        recv_sem=amp_recv.at[r * cols + c], device_id={"row": r, "col": c},
                        device_id_type=MESH,
                    ).wait_recv()

        def own_greens(period, carry):
            greens(period)
            return carry

        @pl.when(row == root)
        def _():
            lax.fori_loop(0, TICKS, own_greens, 0)

        def tick(period, carry):
            @pl.when(row != root)
            def _():
                greens(period)

            @pl.when(row > root)
            def _():
                pass_on(period, 0, row < rows - 1)

            @pl.when(row < root)
            def _():
                pass_on(period, 1, row > 0)

            @pl.when(row == root)
            def _():
                eliminate(period)
                each_tile(period, lambda copy: copy.start(), lambda copy: copy.start())

            return carry

        lax.fori_loop(0, TICKS, tick, 0)

    @pl.when(at_root)
    def _():
        @pl.when(sec < sectors - 1)
        def _():
            for k in range(half_blocks):
                shift_copy(k, 1).wait_send()

        for period in range(TICKS):
            each_tile(period, lambda copy: copy.wait_send(), lambda copy: copy.wait())

    @pl.when(jnp.logical_not(at_root))
    def _():
        for period in range(TICKS):
            pltpu.make_async_remote_copy(
                src_ref=out_ref.at[period],
                dst_ref=out_ref.at[period],
                send_sem=tile_send.at[period, 0],
                recv_sem=tile_recv.at[period],
                device_id={"row": root, "col": home},
                device_id_type=MESH,
            ).wait_recv()


def gather(panels, weight, tiles, rows, cols, sectors):
    _, row_block, states = panels.shape
    chunk = states // rows
    channels = rows * row_block
    pairs = channels // BLOCK
    width = (2 * pairs + 1) * BLOCK
    pieces = len(piece_list(2 * pairs)[0])
    assert row_block == BLOCK and TICKS == 2
    vmem = pl.BlockSpec(memory_space=pltpu.VMEM)
    dma = pltpu.SemaphoreType.DMA
    f32, bf16 = jnp.float32, jnp.bfloat16
    packed = pltpu.VMEM((pairs // 2, BLOCK, (pairs + 1) * BLOCK), f32)
    return pl.pallas_call(
        functools.partial(gather_kernel, rows, cols, sectors),
        out_shape=jax.ShapeDtypeStruct(tiles.shape, f32),
        in_specs=[pl.BlockSpec(memory_space=pl.ANY), vmem, vmem],
        out_specs=vmem,
        scratch_shapes=[
            pltpu.VMEM((2, channels, cols * chunk), bf16),
            pltpu.VMEM((weight.shape[0], cols * chunk), f32),
            pltpu.VMEM((TICKS, channels, BLOCK), f32),
            pltpu.VMEM((2, channels, cols * chunk), bf16),
            pltpu.VMEM((TICKS, pairs, BLOCK, width), f32),
            pltpu.VMEM((TICKS, 2, pairs, BLOCK, width), f32),
            pltpu.VMEM((2 * channels, 2 * channels), f32),
            pltpu.VMEM((BLOCK, BLOCK), f32),
            pltpu.VMEM((TICKS, channels, channels), f32),
            packed,
            packed,
            dma((rows,)),
            dma((rows * cols,)),
            dma((2,)),
            dma((2, cols)),
            dma((TICKS, pieces)),
            dma((TICKS, 2, pieces)),
            dma((TICKS, rows * cols)),
            dma((TICKS,)),
            dma((pairs,)),
            dma((pairs,)),
        ],
        compiler_params=pltpu.CompilerParams(
            collective_id=0, has_side_effects=True, vmem_limit_bytes=52 * 1024 * 1024
        ),
        name="sectors",
    )(panels, weight, tiles)


def local(amplitudes, state_energies, radii_table, plan, entry_r, fresh_r):
    sec_index = lax.axis_index("sec")
    row_index = lax.axis_index("row")
    sectors, rows, cols = (lax.axis_size(axis) for axis in ("sec", "row", "col"))
    panels = amplitudes[0]
    chunk = panels.shape[2] // rows
    levels = lax.dynamic_slice_in_dim(state_energies[0], row_index * chunk, chunk)
    bounds = lax.dynamic_slice_in_dim(radii_table, sec_index, 2)
    sector_width = (bounds[1] - bounds[0]).astype(jnp.float32)
    energies = plan[0].astype(jnp.float32) / ENERGIES
    weight = 8.0 / (sector_width * (levels[None, :] - energies[:, None]))
    weight = jnp.pad(weight, ((0, SUB - TICKS), (0, 0)))
    tiles = jnp.concatenate([entry_r, jnp.where(sec_index == 0, fresh_r, 0.0)], 0)
    return gather(panels, weight, tiles, rows, cols, sectors)[:, None]


def solution(mesh):
    placed = (
        P("sec", None, "row", "col"),
        P("sec", "col"),
        P(),
        P("sec", None),
        P("sec", "col", "row"),
        P(None, "col", "row"),
    )
    return jax.shard_map(
        local, mesh=mesh, in_specs=placed, out_specs=P(None, "sec", "col", "row"), check_vma=False
    )
```

```python
import functools
import jax
import jax.numpy as jnp
from jax import lax
from jax.experimental import pallas as pl
from jax.experimental.pallas import tpu as pltpu
from jax.sharding import PartitionSpec as P

ENERGIES = 32
TICKS = 2
BLOCK = 128
SUB = 8
HIGHEST = lax.Precision.HIGHEST


MESH = pl.DeviceIdType.MESH


def worker(sector):
    return sector % 2


def span(block, blocks):
    if block < blocks // 2:
        return block, 0, (blocks - block) * BLOCK
    mate = blocks - 1 - block
    return mate, (blocks - mate) * BLOCK, (blocks - block) * BLOCK


def piece_list(blocks):
    pieces, of_block = [], []
    for block in range(blocks):
        pair, start, wide = span(block, blocks)
        mine = []
        for first in range(0, wide, 4 * BLOCK):
            mine.append(len(pieces))
            pieces.append((pair, start + first, min(4 * BLOCK, wide - first)))
        of_block.append(mine)
    return pieces, of_block


def inverse_factor(block):
    size = block.shape[0]
    groups = size // SUB
    sub_rows = lax.broadcasted_iota(jnp.int32, (SUB, size), 0)
    left = block
    right = jnp.where(
        lax.broadcasted_iota(jnp.int32, (size, size), 0)
        == lax.broadcasted_iota(jnp.int32, (size, size), 1),
        1.0,
        0.0,
    )
    done = []
    for g in range(groups):
        base = SUB * g
        u, v = left[:SUB], right[:SUB]
        cols = [jnp.broadcast_to(u[:, base + q : base + q + 1], (SUB, size)) for q in range(SUB)]
        scale = jnp.zeros((SUB, size), jnp.float32)
        for p in range(SUB):
            root = lax.rsqrt(cols[p][p : p + 1, :])
            scale = jnp.where(sub_rows == p, root, scale)
            if p + 1 < SUB:
                f = jnp.where(sub_rows > p, cols[p], 0.0) * (root * root)
                u = u - f * u[p : p + 1, :]
                v = v - f * v[p : p + 1, :]
                for q in range(p + 1, SUB):
                    cols[q] = cols[q] - f * cols[q][p : p + 1, :]
        u = u * scale
        v = v * scale
        done.append(v)
        if g + 1 < groups:
            turned = u.T[base + SUB :, :]
            left, right = left[SUB:], right[SUB:]
            for q in range(SUB):
                c = jnp.broadcast_to(turned[:, q : q + 1], turned.shape[:1] + (size,))
                left = left - c * u[q : q + 1, :]
                right = right - c * v[q : q + 1, :]
    return jnp.concatenate(done, 0)


def gather_kernel(
    rows, cols, sectors, amp_ref, weight_ref, tile_ref, out_ref,
    panels, weights, tiles, scaled, parts, arrived, work, factor_ref, full, upper, inbox,
    amp_send, amp_recv, small_send, small_recv, sum_send, sum_recv,
    tile_send, tile_recv, shift_send, shift_recv,
):
    row, col = lax.axis_index("row"), lax.axis_index("col")
    sec = lax.axis_index("sec")
    home = worker(sec)
    root = (rows - 1) // 2
    chunk = weight_ref.shape[1]
    row_block = amp_ref.shape[1]
    tile_rows = tile_ref.shape[1]
    channels = panels.shape[1]
    blocks = 2 * channels // BLOCK
    at_home = col == home
    at_root = at_home & (row == root)

    barrier = pltpu.get_barrier_semaphore()
    for r in range(rows):
        for c in range(cols):

            @pl.when((row != r) | (col != c))
            def _():
                pl.semaphore_signal(
                    barrier, inc=1, device_id={"row": r, "col": c}, device_id_type=MESH
                )

    for step in (-1, 1):

        @pl.when(at_root & (sec + step >= 0) & (sec + step < sectors))
        def _():
            pl.semaphore_signal(
                barrier,
                inc=1,
                device_id={"sec": sec + step, "col": worker(sec + step + 2)},
                device_id_type=MESH,
            )

    before = jnp.where(at_root & (sec > 0), 1, 0)
    after = jnp.where(at_root & (sec < sectors - 1), 1, 0)
    pl.semaphore_wait(barrier, rows * cols - 1 + before + after)

    my_rows = pl.ds(pl.multiple_of(row * row_block, row_block), row_block)
    my_states = pl.ds(pl.multiple_of(col * chunk, chunk), chunk)
    my_tile = pl.ds(pl.multiple_of(col * tile_rows, tile_rows), tile_rows)
    source = row * cols + col

    def amp_there(d):
        r = lax.rem(row + d, rows)
        return pltpu.make_async_remote_copy(
            src_ref=amp_ref.at[:, :, pl.ds(pl.multiple_of(r * chunk, chunk), chunk)],
            dst_ref=panels.at[:, my_rows, my_states],
            send_sem=amp_send.at[d],
            recv_sem=amp_recv.at[source],
            device_id={"row": r, "col": home},
            device_id_type=MESH,
        )

    def amp_here(d):
        r = lax.rem(row + d, rows)
        return pltpu.make_async_copy(
            amp_ref.at[:, :, pl.ds(pl.multiple_of(r * chunk, chunk), chunk)],
            panels.at[:, my_rows, my_states],
            amp_send.at[d],
        )

    def small_there(src, dst, i):
        return pltpu.make_async_remote_copy(
            src_ref=src,
            dst_ref=dst,
            send_sem=small_send.at[i],
            recv_sem=small_recv.at[i, col],
            device_id={"col": home},
            device_id_type=MESH,
        )

    smalls = [
        (weight_ref, weights.at[:, my_states]),
        (tile_ref, tiles.at[:, my_tile, :]),
    ]
    for i, (src, dst) in enumerate(smalls):

        @pl.when(at_home)
        def _():
            pltpu.make_async_copy(src, dst, small_send.at[i]).start()

        @pl.when(jnp.logical_not(at_home))
        def _():
            small_there(src, dst, i).start()

    for d in (*range(1, rows), 0):
        here = at_home & (d == 0)

        @pl.when(here)
        def _():
            amp_here(d).start()

        @pl.when(jnp.logical_not(here))
        def _():
            amp_there(d).start()

    for i, (src, dst) in enumerate(smalls):

        @pl.when(at_home)
        def _():
            pltpu.make_async_copy(src, dst, small_send.at[i]).wait()

        @pl.when(jnp.logical_not(at_home))
        def _():
            small_there(src, dst, i).wait_send()

    for d in (*range(1, rows), 0):
        here = at_home & (d == 0)

        @pl.when(here)
        def _():
            amp_here(d).wait()

        @pl.when(jnp.logical_not(here))
        def _():
            amp_there(d).wait_send()

    pieces, of_block = piece_list(blocks)

    def piece_copy(period, i, side):
        pair, first, wide = pieces[i]
        return pltpu.make_async_remote_copy(
            src_ref=parts.at[period, pair, :, pl.ds(first, wide)],
            dst_ref=arrived.at[period, side, pair, :, pl.ds(first, wide)],
            send_sem=sum_send.at[period, i],
            recv_sem=sum_recv.at[period, side, i],
            device_id={"row": row - 1 if side == 0 else row + 1},
            device_id_type=MESH,
        )

    def piece_arrival(period, i, side):
        pair, first, wide = pieces[i]
        return pltpu.make_async_remote_copy(
            src_ref=parts.at[period, pair, :, pl.ds(first, wide)],
            dst_ref=arrived.at[period, side, pair, :, pl.ds(first, wide)],
            send_sem=sum_send.at[period, i],
            recv_sem=sum_recv.at[period, side, i],
            device_id={"row": row + 1 if side == 0 else row - 1},
            device_id_type=MESH,
        )

    def pass_on(period, side, inner):
        for i, (pair, first, wide) in enumerate(pieces):
            at = slice(first, first + wide)

            @pl.when(inner)
            def _():
                piece_arrival(period, i, side).wait_recv()
                parts[period, pair, :, at] += arrived[period, side, pair, :, at]

            piece_copy(period, i, side).start()
        for i in range(len(pieces)):
            piece_copy(period, i, side).wait_send()

    def take_sums(period, block):
        for i in of_block[block]:
            pair, first, wide = pieces[i]
            total = parts[period, pair, :, first : first + wide]
            if root < rows - 1:
                piece_arrival(period, i, 0).wait_recv()
                total = total + arrived[period, 0, pair, :, first : first + wide]
            if root > 0:
                piece_arrival(period, i, 1).wait_recv()
                total = total + arrived[period, 1, pair, :, first : first + wide]
            at = block * BLOCK + first - span(block, blocks)[1]
            work[block * BLOCK : (block + 1) * BLOCK, at : at + wide] += total

    half_blocks = blocks // 2

    def shift_copy(k, step):
        pair, start, wide = span(k, half_blocks)
        return pltpu.make_async_remote_copy(
            src_ref=upper.at[pair, :, pl.ds(start, wide)],
            dst_ref=inbox.at[pair, :, pl.ds(start, wide)],
            send_sem=shift_send.at[k],
            recv_sem=shift_recv.at[k],
            device_id={"sec": sec + step, "col": worker(sec + step + 2)},
            device_id_type=MESH,
        )

    def tile_copy(period, r, c):
        return pltpu.make_async_remote_copy(
            src_ref=full.at[period, pl.ds(c * tile_rows, tile_rows), pl.ds(r * row_block, row_block)],
            dst_ref=out_ref.at[period],
            send_sem=tile_send.at[period, r * cols + c],
            recv_sem=tile_recv.at[period],
            device_id={"row": r, "col": c},
            device_id_type=MESH,
        )

    def tile_here(period, c):
        return pltpu.make_async_copy(
            full.at[period, pl.ds(c * tile_rows, tile_rows), pl.ds(root * row_block, row_block)],
            out_ref.at[period],
            tile_send.at[period, root * cols + c],
        )

    def each_tile(period, there, here):
        for c in range(cols):
            for r in range(rows):
                if r == root:

                    @pl.when(col == c)
                    def _():
                        here(tile_here(period, c))

                    @pl.when(col != c)
                    def _():
                        there(tile_copy(period, r, c))

                else:
                    there(tile_copy(period, r, c))

    def eliminate(period):
        for block in range(blocks):
            wide = (blocks - block) * BLOCK
            work[block * BLOCK : (block + 1) * BLOCK, block * BLOCK :] = jnp.zeros(
                (BLOCK, wide), jnp.float32
            )

        def step(k, carry):
            for j in range(half_blocks):

                @pl.when(k == j)
                def _():
                    take_sums(period, j)

                @pl.when((k == j) & (period > 0) & (sec > 0))
                def _():
                    shift_copy(j, -1).wait_recv()
                    pair, start, wide = span(j, half_blocks)
                    work[j * BLOCK : (j + 1) * BLOCK, j * BLOCK : channels] += inbox[
                        pair, :, start : start + wide
                    ]

            lo = pl.multiple_of(k * BLOCK, BLOCK)
            factor_ref[...] = inverse_factor(work[pl.ds(lo, BLOCK), pl.ds(lo, BLOCK)])
            for j in range(half_blocks):

                @pl.when(k == j)
                def _():
                    hi = (j + 1) * BLOCK
                    solved = jnp.dot(
                        factor_ref[...],
                        work[j * BLOCK : hi, hi:],
                        precision=HIGHEST,
                        preferred_element_type=jnp.float32,
                    )
                    for i in range(hi, 2 * channels, BLOCK):
                        work[i : i + BLOCK, i:] -= lax.dot_general(
                            solved[:, i - hi : i - hi + BLOCK],
                            solved[:, i - hi :],
                            (((0,), (0,)), ((), ())),
                            precision=HIGHEST,
                            preferred_element_type=jnp.float32,
                        )

            return carry

        lax.fori_loop(0, half_blocks, step, 0)
        for i in range(half_blocks):
            take_sums(period, half_blocks + i)
            lo = channels + i * BLOCK
            pair, start, wide = span(i, half_blocks)

            @pl.when(period == 0)
            def _():
                upper[pair, :, start : start + wide] = work[lo : lo + BLOCK, lo:]

            @pl.when((period == 0) & (sec < sectors - 1))
            def _():
                shift_copy(i, 1).start()

            for j in range(i, half_blocks):
                at = channels + j * BLOCK
                tile = work[lo : lo + BLOCK, at : at + BLOCK]
                full[period, i * BLOCK : (i + 1) * BLOCK, j * BLOCK : (j + 1) * BLOCK] = tile
                if j > i:
                    full[period, j * BLOCK : (j + 1) * BLOCK, i * BLOCK : (i + 1) * BLOCK] = tile.T

    def greens(period):
        weight = weights[pl.ds(period, 1), :]
        for side in range(2):
            scaled[side] = (panels[side].astype(jnp.float32) * weight).astype(jnp.bfloat16)
        contraction = (((1,), (1,)), ((), ()))
        for left, right, first_block, first_column in (
            (0, 0, 0, 0),
            (0, 1, 0, channels),
            (1, 1, channels // BLOCK, channels),
        ):
            for i in range(0, channels, 2 * BLOCK):
                begin = i if left == right else 0
                green = lax.dot_general(
                    scaled[left, i : i + 2 * BLOCK, :],
                    panels[right, begin:, :],
                    contraction,
                    preferred_element_type=jnp.float32,
                )
                for j in range(2):
                    block = first_block + i // BLOCK + j
                    pair, start, _ = span(block, blocks)
                    skip = j * BLOCK if left == right else 0
                    at = start + first_column + begin + skip - block * BLOCK
                    wide = channels - begin - skip
                    parts[period, pair, :, at : at + wide] = green[
                        j * BLOCK : (j + 1) * BLOCK, skip:
                    ]
        for r in range(rows):

            @pl.when(row == r)
            def _():
                for block in range(r + 1):
                    pair, start, _ = span(block, blocks)
                    at = start + (r - block) * BLOCK
                    parts[period, pair, :, at : at + BLOCK] += tiles[
                        period, block * BLOCK : (block + 1) * BLOCK, :
                    ]

    @pl.when(at_home)
    def _():
        for c in range(cols):

            @pl.when(col != c)
            def _():
                for i in range(2):
                    dst = (
                        weights.at[:, pl.ds(c * chunk, chunk)],
                        tiles.at[:, pl.ds(c * tile_rows, tile_rows), :],
                    )[i]
                    pltpu.make_async_remote_copy(
                        src_ref=dst, dst_ref=dst, send_sem=small_send.at[i],
                        recv_sem=small_recv.at[i, c], device_id={"col": c}, device_id_type=MESH,
                    ).wait_recv()

            for r in range(rows):

                @pl.when((row != r) | (col != c))
                def _():
                    dst = panels.at[
                        :, pl.ds(r * row_block, row_block), pl.ds(c * chunk, chunk)
                    ]
                    pltpu.make_async_remote_copy(
                        src_ref=dst, dst_ref=dst, send_sem=amp_send.at[0],
                        recv_sem=amp_recv.at[r * cols + c], device_id={"row": r, "col": c},
                        device_id_type=MESH,
                    ).wait_recv()

        def own_greens(period, carry):
            greens(period)
            return carry

        @pl.when(row == root)
        def _():
            lax.fori_loop(0, TICKS, own_greens, 0)

        def tick(period, carry):
            @pl.when(row != root)
            def _():
                greens(period)

            @pl.when(row > root)
            def _():
                pass_on(period, 0, row < rows - 1)

            @pl.when(row < root)
            def _():
                pass_on(period, 1, row > 0)

            @pl.when(row == root)
            def _():
                eliminate(period)
                each_tile(period, lambda copy: copy.start(), lambda copy: copy.start())

            return carry

        lax.fori_loop(0, TICKS, tick, 0)

    @pl.when(at_root)
    def _():
        @pl.when(sec < sectors - 1)
        def _():
            for k in range(half_blocks):
                shift_copy(k, 1).wait_send()

        for period in range(TICKS):
            each_tile(period, lambda copy: copy.wait_send(), lambda copy: copy.wait())

    @pl.when(jnp.logical_not(at_root))
    def _():
        for period in range(TICKS):
            pltpu.make_async_remote_copy(
                src_ref=out_ref.at[period],
                dst_ref=out_ref.at[period],
                send_sem=tile_send.at[period, 0],
                recv_sem=tile_recv.at[period],
                device_id={"row": root, "col": home},
                device_id_type=MESH,
            ).wait_recv()


def gather(panels, weight, tiles, rows, cols, sectors):
    _, row_block, states = panels.shape
    chunk = states // rows
    channels = rows * row_block
    pairs = channels // BLOCK
    width = (2 * pairs + 1) * BLOCK
    pieces = len(piece_list(2 * pairs)[0])
    assert row_block == BLOCK and TICKS == 2
    vmem = pl.BlockSpec(memory_space=pltpu.VMEM)
    dma = pltpu.SemaphoreType.DMA
    f32, bf16 = jnp.float32, jnp.bfloat16
    packed = pltpu.VMEM((pairs // 2, BLOCK, (pairs + 1) * BLOCK), f32)
    return pl.pallas_call(
        functools.partial(gather_kernel, rows, cols, sectors),
        out_shape=jax.ShapeDtypeStruct(tiles.shape, f32),
        in_specs=[pl.BlockSpec(memory_space=pl.ANY), vmem, vmem],
        out_specs=vmem,
        scratch_shapes=[
            pltpu.VMEM((2, channels, cols * chunk), bf16),
            pltpu.VMEM((weight.shape[0], cols * chunk), f32),
            pltpu.VMEM((TICKS, channels, BLOCK), f32),
            pltpu.VMEM((2, channels, cols * chunk), bf16),
            pltpu.VMEM((TICKS, pairs, BLOCK, width), f32),
            pltpu.VMEM((TICKS, 2, pairs, BLOCK, width), f32),
            pltpu.VMEM((2 * channels, 2 * channels), f32),
            pltpu.VMEM((BLOCK, BLOCK), f32),
            pltpu.VMEM((TICKS, channels, channels), f32),
            packed,
            packed,
            dma((rows,)),
            dma((rows * cols,)),
            dma((2,)),
            dma((2, cols)),
            dma((TICKS, pieces)),
            dma((TICKS, 2, pieces)),
            dma((TICKS, rows * cols)),
            dma((TICKS,)),
            dma((pairs,)),
            dma((pairs,)),
        ],
        compiler_params=pltpu.CompilerParams(
            collective_id=0, has_side_effects=True, vmem_limit_bytes=52 * 1024 * 1024
        ),
        name="sectors",
    )(panels, weight, tiles)


def local(amplitudes, state_energies, radii_table, plan, entry_r, fresh_r):
    sec_index = lax.axis_index("sec")
    row_index = lax.axis_index("row")
    sectors, rows, cols = (lax.axis_size(axis) for axis in ("sec", "row", "col"))
    panels = amplitudes[0]
    chunk = panels.shape[2] // rows
    levels = lax.dynamic_slice_in_dim(state_energies[0], row_index * chunk, chunk)
    bounds = lax.dynamic_slice_in_dim(radii_table, sec_index, 2)
    sector_width = (bounds[1] - bounds[0]).astype(jnp.float32)
    energies = plan[0].astype(jnp.float32) / ENERGIES
    weight = 8.0 / (sector_width * (levels[None, :] - energies[:, None]))
    weight = jnp.pad(weight, ((0, SUB - TICKS), (0, 0)))
    tiles = jnp.concatenate([entry_r, jnp.where(sec_index == 0, fresh_r, 0.0)], 0)
    return gather(panels, weight, tiles, rows, cols, sectors)[:, None]


def solution(mesh):
    placed = (
        P("sec", None, "row", "col"),
        P("sec", "col"),
        P(),
        P("sec", None),
        P("sec", "col", "row"),
        P(None, "col", "row"),
    )
    return jax.shard_map(
        local, mesh=mesh, in_specs=placed, out_specs=P(None, "sec", "col", "row"), check_vma=False
    )
```
